32 devices in a mesh: gx: 4 (over y, x), gy: 8 (over z, core).
Axes of the slice: x: 2, y: 2, z: 4, core: 2. Of those that a mesh axis runs over, the one named last changes fastest.
Arguments:
- a_blocks: bfloat16 [2048, 8, 9216], P(('gx', 'gy')), may hold values from -2 to 2
- a_cols: int32 [2048, 8], P(('gx', 'gy')), may hold values from 0 to 63
- q_blocks: bfloat16 [2048, 9216], P(('gx', 'gy')), may hold values from -0.625 to 0.625
- part_of: int32 [2048, 8], P(('gx', 'gy')), may hold values from 0 to 63
- part_dest: int32 [2048, 1], P(('gx', 'gy')), may hold values from 0 to 7; in each aligned block of 64 rows (0 to 63, 64 to 127, ...) at most 16 rows name the same one
- part_pos: int32 [2048], P(('gx', 'gy')), may hold values from 0 to 15
- g_level: float32 [3, 9216], replicated, may hold values from -0.625 to 0.625
Outputs:
- coarse_first: float32 [64, 8, 9216], P(('gx', 'gy'))
- coarsest: float32 [64, 8, 9216], P(('gx', 'gy'))
The draws below stay inside these ranges and needn't reach their ends.
Inputs may be any that keep to these rules, and one draw needn't show every extreme that they name: `part_dest`: among the partial blocks of one device at most 16 name the same gy index, and some device's blocks name one index exactly 16 times.
All inputs are finite; a program needn't handle non-finite values.
Results may differ from the reference program's by a relative error of at most 0.0029.
Values sent between devices are 32-bit elements; how exact they have to be, the bound alone decides.
A program may use at most 128 MiB of HBM per device.

```python
import math
import jax
import jax.numpy as jnp
import numpy as np
from jax import lax

B = 96
R = 64
KA = 8
RC = 2
SC = 8
NP = 64
CAP = 16
FINE = 2048
N_GX = 4
N_GY = 8


def set_ends(drawn, own_key, smallest, top_value):
    longest = drawn.shape.index(max(drawn.shape))
    spots = []
    for shift in (0, 1):
        where = [jax.random.randint(jax.random.fold_in(own_key, axis), (), 0, length) for axis, length in enumerate(drawn.shape)]
        where[longest] = (where[longest] + shift) % drawn.shape[longest]
        spots.append(tuple(where))
    return drawn.at[spots[0]].set(smallest).at[spots[1]].set(top_value)


def levels(rng, shape, cuts, low, largest):
    def one(axis_at, blocks):
        heights = jax.random.uniform(jax.random.fold_in(jax.random.fold_in(rng, 6), axis_at), (blocks,), jnp.float32, low / len(cuts), largest / len(cuts))
        return jnp.repeat(jnp.exp(heights), shape[axis_at] // blocks).reshape((-1,) + (1,) * (len(shape) - axis_at - 1))

    gain = one(*cuts[0])
    for cut in cuts[1:]:
        gain = gain * one(*cut)
    return gain


def shared_out(stream_key, own, number, rows, number_of, top, limit, skew):
    ranking = jax.random.permutation(stream_key, number_of)
    crowded, common = load_shares(number_of, rows * top, limit, skew, True), load_shares(number_of, rows * top, limit, skew, False)
    places = jnp.arange(number_of)

    def named(sizes, offset_by):
        used = int((sizes > 0).sum())
        fixed = max(1, used // 4)
        passed = fixed + (places - fixed + offset_by * (used - fixed)) % max(1, number_of - fixed)
        return jnp.zeros((number_of,), jnp.int32).at[ranking[jnp.where(places < fixed, places, passed)]].set(jnp.asarray(sizes, jnp.int32))

    sizes = jnp.where(number % 4 == 0, named(crowded, number // 4), named(common, number - number // 4 - 1))
    mixed = jax.random.permutation(jax.random.fold_in(own, 3), number_of)
    donor, taker = mixed[0:number_of // 2 * 2:2], mixed[1:number_of // 2 * 2:2]
    slack = jnp.minimum(sizes[donor] - 1, limit - sizes[taker]) // 2
    slack = jnp.where((donor == ranking[0]) | (taker == ranking[0]) | (sizes[taker] == 0), 0, jnp.maximum(slack, 0))
    passed = jax.random.randint(jax.random.fold_in(own, 4), (number_of // 2,), 0, 1 << 20) % (slack + 1)
    sizes = sizes.at[donor].add(-passed).at[taker].add(passed)
    members = jnp.searchsorted(jnp.cumsum(sizes), jnp.arange(rows * top), side="right").astype(jnp.int32)
    table = members.reshape(top, rows).T
    table = table[jax.random.permutation(jax.random.fold_in(own, 1), rows)]
    offset_by = jax.random.randint(jax.random.fold_in(own, 2), (rows, 1), 0, top)
    return jnp.take_along_axis(table, (jnp.arange(top)[None, :] + offset_by) % top, axis=1)


def load_shares(amount, total, bound, lean, full):
    loads = [(1 << 20) // math.isqrt(standing ** lean) + 1 for standing in range(1, amount + 1)]
    largest = bound if full else min(bound, max(-(-total // amount), total * loads[0] // sum(loads)))
    least = 1 if total - largest >= amount - 1 else 0
    holding, surplus = [largest] + [least] * (amount - 1), total - largest - least * (amount - 1)
    while surplus > 0:
        movable = [i for i in range(1, amount) if holding[i] < largest] or [i for i in range(1, amount) if holding[i] < bound]
        whole, left = sum([loads[i] for i in movable]), surplus
        for i in movable:
            extra = min(bound - holding[i], max(1, left * loads[i] // whole), surplus)
            holding[i] = holding[i] + extra
            surplus = surplus - extra
    return np.array(holding)


def bell_draw(stream_key, extent, scale, reach, shards=(), kind=jnp.bfloat16):
    gain = levels(stream_key, extent, shards, -0.22, 0.18) if shards else 1.0
    drawn = jax.random.normal(stream_key, extent, jnp.float32) * scale * gain
    return jnp.minimum(jnp.maximum(drawn, -reach), reach).astype(kind)


def setup_inputs(seed: int = 0) -> dict:
    key_list = jax.random.split(jax.random.key(seed), 8)
    a_blocks = bell_draw(key_list[0], (FINE, KA, B * B), 0.15, 2.0, ((0, 32),))
    a_cols = set_ends(jax.random.randint(key_list[1], (FINE, KA), 0, R), jax.random.fold_in(key_list[1], 1), 0, R - 1).astype(jnp.int32)
    q_blocks = bell_draw(key_list[2], (FINE, B * B), B ** -0.5, 0.625, ((0, 32),))
    part_of = set_ends(jax.random.randint(key_list[3], (FINE, KA), 0, NP), jax.random.fold_in(key_list[3], 1), 0, NP - 1).astype(jnp.int32)
    part_dest_keys = jax.random.split(jax.random.fold_in(key_list[4], 1), (NP * N_GX * N_GY) // NP)
    part_dest_turns = jax.random.permutation(jax.random.fold_in(key_list[4], 3), (NP * N_GX * N_GY) // NP)
    part_dest = jax.vmap(lambda own, number: shared_out(jax.random.fold_in(key_list[4], 2), own, number, NP, N_GY, 1, CAP, 2))(part_dest_keys, part_dest_turns).reshape((NP * N_GX * N_GY, 1))
    part_pos = set_ends(jax.random.randint(key_list[5], (NP * N_GX * N_GY,), 0, RC * SC), jax.random.fold_in(key_list[5], 1), 0, (RC * SC) - 1).astype(jnp.int32)
    g_level = bell_draw(key_list[6], (3, B * B), B ** -0.5, 0.625, (), jnp.float32)
    return {"a_blocks": a_blocks, "a_cols": a_cols, "q_blocks": q_blocks, "part_of": part_of, "part_dest": part_dest, "part_pos": part_pos, "g_level": g_level}


def project(blocks, gmat):
    right = jnp.einsum('...ab,bj->...aj', blocks, gmat, precision=lax.Precision.HIGHEST)
    return jnp.einsum('ai,...aj->...ij', gmat, right, precision=lax.Precision.HIGHEST)


def reference(a_blocks, a_cols, q_blocks, part_of, part_dest, part_pos, g_level):
    ndev = N_GX * N_GY
    cells = RC * SC
    width = B * B
    a_all = a_blocks.reshape(ndev, R, KA, B, B)
    c_all = a_cols.reshape(ndev, R, KA)
    q_all = q_blocks.reshape(ndev, R, B, B)
    p_all = part_of.reshape(ndev, R * KA)
    dst_all = part_dest.reshape(ndev, NP)
    pos_all = part_pos.reshape(ndev, NP)
    ids = jnp.arange(ndev, dtype=jnp.int32)

    def step(carry, items):
        a_dev, c_dev, q_dev, p_dev, dst_dev, pos_dev, dev = items
        qfull = q_dev.astype(jnp.float32)
        picked = qfull[c_dev]
        aq_rows = jnp.einsum('rkij,rkjl->rkil', a_dev.astype(jnp.float32), picked).astype(jnp.bfloat16)
        terms = jnp.einsum('rji,rkjl->rkil', qfull, aq_rows.astype(jnp.float32))
        partial_value = jax.ops.segment_sum(terms.reshape(R * KA, width), p_dev, num_segments=NP)
        target = (((dev // N_GY) * N_GY + dst_dev) * cells + pos_dev).astype(jnp.int32)
        return carry.at[target].add(partial_value), None

    start = jnp.zeros((ndev * cells, width), jnp.float32)
    total, _ = lax.scan(step, start, (a_all, c_all, q_all, p_all, dst_all, pos_all, ids))
    coarse_first = total.reshape(ndev * RC, SC, width)
    gmats = g_level.reshape(3, B, B)
    level = total.reshape(N_GX, N_GY, cells, B, B)
    level = project(level.reshape(N_GX, N_GY // 2, 2, cells, B, B).sum(2), gmats[0])
    level = project(level.reshape(N_GX, N_GY // 4, 2, cells, B, B).sum(2), gmats[1])
    level = project(level.sum(0), gmats[2])
    spread = jnp.broadcast_to(level[None, :, None], (N_GX, N_GY // 4, 4, cells, B, B))
    coarsest = spread.reshape(ndev * RC, SC, width)
    return coarse_first, coarsest
```

```python
import functools

import jax
import jax.numpy as jnp
from jax import lax
from jax.experimental import pallas as pl
from jax.experimental.pallas import tpu as pltpu
from jax.sharding import PartitionSpec as P

B = 96
L = 128
G = 24
RC = 2
SC = 8
ROWS = 8
F32 = jnp.float32
BF16 = jnp.bfloat16


def lanes():
    return lax.broadcasted_iota(jnp.int32, (G, L), 1)


def split_rows(t):
    lane = lanes()
    return [
        t[0],
        pltpu.roll(jnp.where(lane >= 96, t[0], t[1]), 32, 1),
        pltpu.roll(jnp.where(lane >= 64, t[1], t[2]), 64, 1),
        pltpu.roll(t[2], 96, 1),
    ]


def join_rows(c):
    lane = lanes()
    one = pltpu.roll(c[1], 96, 1)
    two = pltpu.roll(c[2], 64, 1)
    three = pltpu.roll(c[3], 32, 1)
    return [
        jnp.where(lane < 96, c[0], one),
        jnp.where(lane < 64, one, two),
        jnp.where(lane < 32, two, three),
    ]


def tiles(ref, at, pitch):
    return [ref[pl.ds(m * pitch + at, G, stride=3 * pitch), :] for m in range(3)]


def products_kernel(
    a_ref, q_ref, g_ref, cols_ref, part_ref, dest_ref, pos_ref, dense_ref, h_ref, a_flat, q_flat, g_flat, nat, q_nat, q_tr, acc
):
    step = pl.program_id(0)
    fine = q_ref.shape[0]
    slots = a_ref.shape[1]
    n_part = acc.shape[0]
    width = a_ref.shape[2] // L

    @pl.when(step == 0)
    def _():
        for u in range(width):
            q_flat[u * fine : (u + 1) * fine, :] = q_ref[:, u * L : (u + 1) * L].astype(F32)
            g_flat[u * 8 : u * 8 + 3, :] = g_ref[:, u * L : (u + 1) * L]
        keep = lax.broadcasted_iota(jnp.int32, (B, L), 1) < B
        q_nat[:, B:, :] = jnp.zeros((fine, L - B, L), BF16)

        def one_q(i, _):
            rows = split_rows(tiles(q_flat, i, fine))
            for r in range(4):
                nat[pl.ds(r, G, stride=4), :] = rows[r]
            q_nat[i, :B, :] = jnp.where(keep, nat[...], 0.0).astype(BF16)
            permuted = jnp.concatenate(rows, axis=0)
            q_tr[i] = jnp.transpose(permuted)[:B].astype(BF16)
            return 0

        lax.fori_loop(0, fine, one_q, 0)

        mats = []
        for l in range(3):
            rows = split_rows(tiles(g_flat, l, 8))
            for r in range(4):
                nat[pl.ds(r, G, stride=4), :] = rows[r]
            mats.append(nat[...][:, :B])
        h = jnp.dot(mats[0], mats[1], precision=lax.Precision.HIGHEST, preferred_element_type=F32)
        h_ref[...] = jnp.dot(h, mats[2], precision=lax.Precision.HIGHEST, preferred_element_type=F32)

        def clear(p, _):
            acc[p] = jnp.zeros((B, L), F32)
            return 0

        lax.fori_loop(0, n_part, clear, 0)

        def clear_dense(p, _):
            dense_ref[pl.ds(p * 128, 128), :] = jnp.zeros((128, L), F32)
            return 0

        lax.fori_loop(0, dense_ref.shape[0] // 128, clear_dense, 0)

    def one_row(rr, slot):
        i = step * ROWS + rr
        flat = a_flat.at[slot]
        for u in range(width):
            flat[u * slots : (u + 1) * slots, :] = a_ref[rr, :, u * L : (u + 1) * L].astype(F32)
        made = []
        for k in range(slots):
            block = jnp.concatenate(split_rows(tiles(flat, k, slots)), axis=0).astype(BF16)
            made.append(jnp.dot(block, q_nat[cols_ref[i, k]], preferred_element_type=F32).astype(BF16))
        term = jnp.dot(q_tr[i], jnp.concatenate(made, axis=1), preferred_element_type=F32)
        for k in range(slots):
            p = part_ref[i, k]
            acc[p] += term[:, k * L : (k + 1) * L]

    def pair(j, _):
        one_row(2 * j, 0)
        one_row(2 * j + 1, 1)
        return 0

    lax.fori_loop(0, ROWS // 2, pair, 0)

    @pl.when(step == pl.num_programs(0) - 1)
    def _():
        cell_rows = width * SC

        def one_part(p, _):
            place = pos_ref[p]
            base = (dest_ref[p, 0] * RC + place // SC) * cell_rows + lax.rem(place, SC)
            flat = join_rows([acc[p, pl.ds(r, G, stride=4), :] for r in range(4)])
            for m in range(3):
                where = pl.ds(base + m * SC, G, stride=3 * SC)
                dense_ref[where, :] = dense_ref[where, :] + flat[m]
            return 0

        lax.fori_loop(0, n_part, one_part, 0)


def products(a_blocks, a_cols, q_blocks, part_of, part_dest, part_pos, g_level, n_inner):
    fine, slots, flat = a_blocks.shape
    n_part = part_pos.shape[0]
    width = flat // L
    smem = pl.BlockSpec(memory_space=pltpu.SMEM)
    vmem = pl.BlockSpec(memory_space=pltpu.VMEM)
    return pl.pallas_call(
        products_kernel,
        grid=(fine // ROWS,),
        out_shape=(
            jax.ShapeDtypeStruct((n_inner * RC * SC * width, L), F32),
            jax.ShapeDtypeStruct((B, B), F32),
        ),
        in_specs=[
            pl.BlockSpec((ROWS, slots, flat), lambda s: (s, 0, 0)),
            vmem,
            vmem,
            smem,
            smem,
            smem,
            smem,
        ],
        out_specs=(vmem, vmem),
        scratch_shapes=[
            pltpu.VMEM((2, width * slots, L), F32),
            pltpu.VMEM((width * fine, L), F32),
            pltpu.VMEM((width * 8, L), F32),
            pltpu.VMEM((B, L), F32),
            pltpu.VMEM((fine, L, L), BF16),
            pltpu.VMEM((fine, B, B), BF16),
            pltpu.VMEM((n_part, B, L), F32),
        ],
        compiler_params=pltpu.CompilerParams(dimension_semantics=("arbitrary",), vmem_limit_bytes=56 * 2**20),
        cost_estimate=pl.CostEstimate(flops=4 * fine * slots * B**3, bytes_accessed=a_blocks.size * 2, transcendentals=0),
    )(a_blocks, q_blocks, g_level, a_cols, part_of, part_dest, part_pos)


def partner_2(shard, axis, stride):
    return lax.ppermute(shard, axis, [(i, i ^ 1 << stride) for i in range(lax.axis_size(axis))])


def local(a_blocks, a_cols, q_blocks, part_of, part_dest, part_pos, g_level):
    flat = a_blocks.shape[2]
    width = flat // L
    n_inner = lax.axis_size("gy")
    dense, h = products(a_blocks, a_cols, q_blocks, part_of, part_dest, part_pos, g_level, n_inner)
    coarse = lax.psum_scatter(dense, "gy", scatter_dimension=0, tiled=True)
    first = coarse.reshape(RC, width, SC, L).transpose(0, 2, 1, 3).reshape(RC, SC, flat)
    total = lax.psum(coarse, "gx")
    for bit in range(2):
        total = total + partner_2(total, "gy", bit)
    total = total.reshape(RC, width, SC, L).transpose(0, 2, 1, 3).reshape(RC * SC, B, B)
    right = jnp.einsum("mab,bj->maj", total, h, precision=lax.Precision.HIGHEST)
    last = jnp.einsum("ai,maj->mij", h, right, precision=lax.Precision.HIGHEST)
    return first, last.reshape(RC, SC, flat)


def solution(mesh):
    placed = (
        P(("gx", "gy"), None, None),
        P(("gx", "gy"), None),
        P(("gx", "gy"), None),
        P(("gx", "gy"), None),
        P(("gx", "gy"), None),
        P(("gx", "gy")),
        P(),
    )
    return jax.shard_map(
        local,
        mesh=mesh,
        in_specs=placed,
        out_specs=(P(("gx", "gy"), None, None), P(("gx", "gy"), None, None)),
        check_vma=False,
    )
```

```python
import functools

import jax
import jax.numpy as jnp
from jax import lax
from jax.experimental import pallas as pl
from jax.experimental.pallas import tpu as pltpu
from jax.sharding import PartitionSpec as P

B = 96
L = 128
G = 24
RC = 2
SC = 8
ROWS = 8
F32 = jnp.float32
BF16 = jnp.bfloat16


def lanes():
    return lax.broadcasted_iota(jnp.int32, (G, L), 1)


def split_rows(t):
    lane = lanes()
    return [
        t[0],
        pltpu.roll(jnp.where(lane >= 96, t[0], t[1]), 32, 1),
        pltpu.roll(jnp.where(lane >= 64, t[1], t[2]), 64, 1),
        pltpu.roll(t[2], 96, 1),
    ]


def join_rows(c):
    lane = lanes()
    one = pltpu.roll(c[1], 96, 1)
    two = pltpu.roll(c[2], 64, 1)
    three = pltpu.roll(c[3], 32, 1)
    return [
        jnp.where(lane < 96, c[0], one),
        jnp.where(lane < 64, one, two),
        jnp.where(lane < 32, two, three),
    ]


def tiles(ref, at, pitch):
    return [ref[pl.ds(m * pitch + at, G, stride=3 * pitch), :] for m in range(3)]


def products_kernel(
    a_ref, q_ref, g_ref, cols_ref, part_ref, dest_ref, pos_ref, dense_ref, h_ref, ht_ref, a_flat, q_flat, g_flat, nat, q_nat, q_tr, acc
):
    step = pl.program_id(0)
    fine = q_ref.shape[0]
    slots = a_ref.shape[1]
    n_part = acc.shape[0]
    width = a_ref.shape[2] // L

    @pl.when(step == 0)
    def _():
        for u in range(width):
            q_flat[u * fine : (u + 1) * fine, :] = q_ref[:, u * L : (u + 1) * L].astype(F32)
            g_flat[u * 8 : u * 8 + 3, :] = g_ref[:, u * L : (u + 1) * L]
        keep = lax.broadcasted_iota(jnp.int32, (B, L), 1) < B
        q_nat[:, B:, :] = jnp.zeros((fine, L - B, L), BF16)

        def one_q(i, _):
            rows = split_rows(tiles(q_flat, i, fine))
            for r in range(4):
                nat[pl.ds(r, G, stride=4), :] = rows[r]
            q_nat[i, :B, :] = jnp.where(keep, nat[...], 0.0).astype(BF16)
            permuted = jnp.concatenate(rows, axis=0)
            q_tr[i] = jnp.transpose(permuted)[:B].astype(BF16)
            return 0

        lax.fori_loop(0, fine, one_q, 0)

        mats = []
        for l in range(3):
            rows = split_rows(tiles(g_flat, l, 8))
            for r in range(4):
                nat[pl.ds(r, G, stride=4), :] = rows[r]
            mats.append(nat[...][:, :B])
        h = jnp.dot(mats[0], mats[1], precision=lax.Precision.HIGHEST, preferred_element_type=F32)
        h = jnp.dot(h, mats[2], precision=lax.Precision.HIGHEST, preferred_element_type=F32)
        h_ref[...] = jnp.zeros((L, L), F32)
        h_ref[:B, :B] = h
        nat[:, :B] = h
        ht_ref[...] = jnp.transpose(jnp.concatenate([nat[pl.ds(r, G, stride=4), :] for r in range(4)], axis=0))[:B]

        def clear(p, _):
            acc[p] = jnp.zeros((B, L), F32)
            return 0

        lax.fori_loop(0, n_part, clear, 0)

        def clear_dense(p, _):
            dense_ref[pl.ds(p * 128, 128), :] = jnp.zeros((128, L), F32)
            return 0

        lax.fori_loop(0, dense_ref.shape[0] // 128, clear_dense, 0)

    def one_row(rr, slot):
        i = step * ROWS + rr
        flat = a_flat.at[slot]
        for u in range(width):
            flat[u * slots : (u + 1) * slots, :] = a_ref[rr, :, u * L : (u + 1) * L].astype(F32)
        made = []
        for k in range(slots):
            block = jnp.concatenate(split_rows(tiles(flat, k, slots)), axis=0).astype(BF16)
            made.append(jnp.dot(block, q_nat[cols_ref[i, k]], preferred_element_type=F32).astype(BF16))
        term = jnp.dot(q_tr[i], jnp.concatenate(made, axis=1), preferred_element_type=F32)
        for k in range(slots):
            p = part_ref[i, k]
            acc[p] += term[:, k * L : (k + 1) * L]

    def pair(j, _):
        one_row(2 * j, 0)
        one_row(2 * j + 1, 1)
        return 0

    lax.fori_loop(0, ROWS // 2, pair, 0)

    @pl.when(step == pl.num_programs(0) - 1)
    def _():
        cell_rows = width * SC

        def one_part(p, _):
            place = pos_ref[p]
            base = (dest_ref[p, 0] * RC + place // SC) * cell_rows + lax.rem(place, SC)
            flat = join_rows([acc[p, pl.ds(r, G, stride=4), :] for r in range(4)])
            for m in range(3):
                where = pl.ds(base + m * SC, G, stride=3 * SC)
                dense_ref[where, :] = dense_ref[where, :] + flat[m]
            return 0

        lax.fori_loop(0, n_part, one_part, 0)


def products(a_blocks, a_cols, q_blocks, part_of, part_dest, part_pos, g_level, n_inner):
    fine, slots, flat = a_blocks.shape
    n_part = part_pos.shape[0]
    width = flat // L
    smem = pl.BlockSpec(memory_space=pltpu.SMEM)
    vmem = pl.BlockSpec(memory_space=pltpu.VMEM)
    return pl.pallas_call(
        products_kernel,
        grid=(fine // ROWS,),
        out_shape=(
            jax.ShapeDtypeStruct((n_inner * RC * SC * width, L), F32),
            jax.ShapeDtypeStruct((L, L), F32),
            jax.ShapeDtypeStruct((B, B), F32),
        ),
        in_specs=[
            pl.BlockSpec((ROWS, slots, flat), lambda s: (s, 0, 0)),
            vmem,
            vmem,
            smem,
            smem,
            smem,
            smem,
        ],
        out_specs=(vmem, vmem, vmem),
        scratch_shapes=[
            pltpu.VMEM((2, width * slots, L), F32),
            pltpu.VMEM((width * fine, L), F32),
            pltpu.VMEM((width * 8, L), F32),
            pltpu.VMEM((B, L), F32),
            pltpu.VMEM((fine, L, L), BF16),
            pltpu.VMEM((fine, B, B), BF16),
            pltpu.VMEM((n_part, B, L), F32),
        ],
        compiler_params=pltpu.CompilerParams(dimension_semantics=("arbitrary",), vmem_limit_bytes=56 * 2**20),
        cost_estimate=pl.CostEstimate(flops=4 * fine * slots * B**3, bytes_accessed=a_blocks.size * 2, transcendentals=0),
    )(a_blocks, q_blocks, g_level, a_cols, part_of, part_dest, part_pos)


def merge_kernel(
    n_gx, pieces, dense, h_ref, ht_ref, first_ref, last_ref, own, pair, right, left, half, other, parts, full, done, nat, local_sem,
    pair_send, pair_recv, right_send, right_recv, left_send, left_recv, core_send, core_recv, part_send, part_recv, full_send, full_recv,
):
    gx = lax.axis_index("gx")
    gy = lax.axis_index("gy")
    n = own.shape[0]
    core, z = lax.rem(gy, 2), gy // 2
    owned = own.shape[1]
    cell_rows = owned // RC
    piece = owned // pieces
    peers = n_gx * 2
    share = cell_rows // peers
    rank = gx * 2 + lax.rem(z, 2)

    def remote(src, dst, send, recv, x, y):
        return pltpu.make_async_remote_copy(
            src_ref=src, dst_ref=dst, send_sem=send, recv_sem=recv, device_id=(x, y), device_id_type=pl.DeviceIdType.MESH
        )

    def peer(offset):
        other_rank = lax.rem(rank + offset, peers)
        return other_rank, other_rank // 2, (z // 2 * 2 + lax.rem(other_rank, 2)) * 2 + core

    barrier = pltpu.get_barrier_semaphore()

    def greet(x, y):
        pl.semaphore_signal(barrier, inc=1, device_id=(x, y), device_id_type=pl.DeviceIdType.MESH)

    partner = gy + 1 - 2 * core
    greet(gx, partner)

    @pl.when(z > 0)
    def _():
        greet(gx, gy - 2)

    @pl.when(z < n - 1)
    def _():
        greet(gx, gy + 2)

    for offset in range(1, peers):
        _, x, y = peer(offset)
        greet(x, y)

    def keep(d):
        return pltpu.make_async_copy(dense.at[2 * d + core], own.at[d], local_sem.at[d])

    def give(d):
        return remote(dense.at[2 * d + 1 - core], pair.at[d], pair_send.at[d], pair_recv.at[d], gx, partner)

    order = [d for t in range(n) for d in (n - 1 - t, t)][:n]
    for d in order:
        keep(d).start()
    pl.semaphore_wait(barrier, peers + (z > 0).astype(jnp.int32) + (z < n - 1).astype(jnp.int32))
    for d in order:
        give(d).start()

    def go_right(d, c):
        rows = pl.ds(c * piece, piece)
        return remote(own.at[d, rows], right.at[d, rows], right_send.at[d, c], right_recv.at[d, c], gx, gy + 2)

    def go_left(d, c):
        rows = pl.ds(c * piece, piece)
        return remote(own.at[d, rows], left.at[d, rows], left_send.at[d, c], left_recv.at[d, c], gx, gy - 2)

    def arrive(d):
        keep(d).wait()
        give(d).wait_recv()

    def step(s, _):
        t, c = s // pieces, lax.rem(s, pieces)
        rows = pl.ds(pl.multiple_of(c * piece, 8), piece)
        far, near = n - 1 - t, t

        @pl.when(z < far)
        def _():
            @pl.when(c == 0)
            def _():
                arrive(far)

            own[far, rows] = own[far, rows] + pair[far, rows]

            @pl.when(z > 0)
            def _():
                go_right(far, c).wait_recv()
                own[far, rows] = own[far, rows] + right[far, rows]

            go_right(far, c).start()

        @pl.when(z > near)
        def _():
            @pl.when(c == 0)
            def _():
                arrive(near)

            own[near, rows] = own[near, rows] + pair[near, rows]

            @pl.when(z < n - 1)
            def _():
                go_left(near, c).wait_recv()
                own[near, rows] = own[near, rows] + left[near, rows]

            go_left(near, c).start()

        return 0

    lax.fori_loop(0, (n - 1) * pieces, step, 0)

    arrive(z)
    own[z] = own[z] + pair[z]

    @pl.when(z < n - 1)
    def _():
        for c in range(pieces):
            go_left(z, c).wait_recv()
        own[z] = own[z] + left[z]

    @pl.when(z > 0)
    def _():
        for c in range(pieces):
            go_right(z, c).wait_recv()
        own[z] = own[z] + right[z]

    mine = pl.ds(pl.multiple_of(core * cell_rows, 8), cell_rows)
    theirs = pl.ds(pl.multiple_of((1 - core) * cell_rows, 8), cell_rows)
    swap = remote(own.at[z, theirs], other, core_send.at[0], core_recv.at[0], gx, partner)
    swap.start()
    swap.wait_recv()
    half[...] = own[z, mine] + other[...]

    def scatter(offset):
        to, x, y = peer(offset)
        rows = pl.ds(pl.multiple_of(to * share, 8), share)
        return remote(half.at[rows], parts.at[peers - offset - 1], part_send.at[offset - 1], part_recv.at[peers - offset - 1], x, y)

    def scattered(offset):
        _, x, y = peer(offset)
        rows = pl.ds(0, share)
        return remote(half.at[rows], parts.at[offset - 1], part_send.at[offset - 1], part_recv.at[offset - 1], x, y)

    for offset in range(1, peers):
        scatter(offset).start()

    for u in range(cell_rows // SC):
        for r in range(RC):
            first_ref[r, :, u * L : (u + 1) * L] = own[z, r * cell_rows + u * SC : r * cell_rows + (u + 1) * SC, :]

    here = pl.ds(pl.multiple_of(rank * share, 8), share)
    total = half[here]
    for offset in range(1, peers):
        scattered(offset).wait_recv()
        total = total + parts[offset - 1]
    full[here] = total

    def gather(offset):
        _, x, y = peer(offset)
        return remote(full.at[here], full.at[here], full_send.at[offset - 1], full_recv.at[peers - offset - 1], x, y)

    def gathered(offset):
        source, x, y = peer(offset)
        rows = pl.ds(pl.multiple_of(source * share, 8), share)
        return remote(full.at[rows], full.at[rows], full_send.at[offset - 1], full_recv.at[offset - 1], x, y)

    for offset in range(1, peers):
        gather(offset).start()
    for offset in range(1, peers):
        gathered(offset).wait_recv()

    blocks = jnp.concatenate([row for s in range(SC) for row in split_rows(tiles(full, s, SC))], axis=0)
    dot = functools.partial(jnp.dot, precision=lax.Precision.HIGHEST, preferred_element_type=F32)
    after = dot(blocks, h_ref[...])
    after = dot(ht_ref[...], jnp.concatenate([after[s * B : (s + 1) * B] for s in range(SC)], axis=1))
    for s in range(SC):
        nat[s] = after[:, s * L : (s + 1) * L]
        flat = join_rows([nat[s, pl.ds(r, G, stride=4), :] for r in range(4)])
        for m in range(3):
            done[core, pl.ds(m * SC + s, G, stride=3 * SC), :] = flat[m]

    finish = remote(done.at[core], done.at[core], core_send.at[1], core_recv.at[1], gx, partner)
    finish.start()
    finished = remote(done.at[1 - core], done.at[1 - core], core_send.at[1], core_recv.at[1], gx, partner)
    finished.wait_recv()
    for u in range(cell_rows // SC):
        for r in range(RC):
            last_ref[r, :, u * L : (u + 1) * L] = done[r, u * SC : (u + 1) * SC, :]

    finish.wait_send()
    swap.wait_send()
    for offset in range(1, peers):
        scatter(offset).wait_send()
        gather(offset).wait_send()
    for d in range(n):
        give(d).wait_send()

        @pl.when(z < d)
        def _():
            for c in range(pieces):
                go_right(d, c).wait_send()

        @pl.when(z > d)
        def _():
            for c in range(pieces):
                go_left(d, c).wait_send()


def merge(dense, h, ht, n_gx, n_inner, flat):
    pieces = 4
    n = n_inner // 2
    peers = n_gx * 2
    owned = dense.shape[0] // n_inner
    cell_rows = owned // RC
    vmem = pl.BlockSpec(memory_space=pltpu.VMEM)
    dma = pltpu.SemaphoreType.DMA
    out = jax.ShapeDtypeStruct((RC, SC, flat), F32)
    return pl.pallas_call(
        functools.partial(merge_kernel, n_gx, pieces),
        out_shape=(out, out),
        in_specs=[pl.BlockSpec(memory_space=pl.ANY), vmem, vmem],
        out_specs=(vmem, vmem),
        scratch_shapes=[pltpu.VMEM((n, owned, L), F32)] * 4
        + [
            pltpu.VMEM((cell_rows, L), F32),
            pltpu.VMEM((cell_rows, L), F32),
            pltpu.VMEM((peers - 1, cell_rows // peers, L), F32),
            pltpu.VMEM((cell_rows, L), F32),
            pltpu.VMEM((RC, cell_rows, L), F32),
            pltpu.VMEM((SC, B, L), F32),
            dma((n,)),
            dma((n,)),
            dma((n,)),
            dma((n, pieces)),
            dma((n, pieces)),
            dma((n, pieces)),
            dma((n, pieces)),
            dma((2,)),
            dma((2,)),
            dma((peers - 1,)),
            dma((peers - 1,)),
            dma((peers - 1,)),
            dma((peers - 1,)),
        ],
        compiler_params=pltpu.CompilerParams(collective_id=0, has_side_effects=True, vmem_limit_bytes=56 * 2**20),
        cost_estimate=pl.CostEstimate(flops=4 * RC * SC * B**3, bytes_accessed=dense.size * 4, transcendentals=0),
    )(dense.reshape(n_inner, owned, L), h, ht)


def local(a_blocks, a_cols, q_blocks, part_of, part_dest, part_pos, g_level):
    n_gx, n_inner = lax.axis_size("gx"), lax.axis_size("gy")
    dense, h, ht = products(a_blocks, a_cols, q_blocks, part_of, part_dest, part_pos, g_level, n_inner)
    return merge(dense, h, ht, n_gx, n_inner, a_blocks.shape[2])


def solution(mesh):
    placed = (
        P(("gx", "gy"), None, None),
        P(("gx", "gy"), None),
        P(("gx", "gy"), None),
        P(("gx", "gy"), None),
        P(("gx", "gy"), None),
        P(("gx", "gy")),
        P(),
    )
    return jax.shard_map(
        local,
        mesh=mesh,
        in_specs=placed,
        out_specs=(P(("gx", "gy"), None, None), P(("gx", "gy"), None, None)),
        check_vma=False,
    )
```

```python
import functools

import jax
import jax.numpy as jnp
from jax import lax
from jax.experimental import pallas as pl
from jax.experimental.pallas import tpu as pltpu
from jax.sharding import PartitionSpec as P

B = 96
L = 128
G = 24
RC = 2
SC = 8
ROWS = 8
F32 = jnp.float32
BF16 = jnp.bfloat16


def lanes():
    return lax.broadcasted_iota(jnp.int32, (G, L), 1)


def split_rows(t):
    lane = lanes()
    return [
        t[0],
        pltpu.roll(jnp.where(lane >= 96, t[0], t[1]), 32, 1),
        pltpu.roll(jnp.where(lane >= 64, t[1], t[2]), 64, 1),
        pltpu.roll(t[2], 96, 1),
    ]


def join_rows(c):
    lane = lanes()
    one = pltpu.roll(c[1], 96, 1)
    two = pltpu.roll(c[2], 64, 1)
    three = pltpu.roll(c[3], 32, 1)
    return [
        jnp.where(lane < 96, c[0], one),
        jnp.where(lane < 64, one, two),
        jnp.where(lane < 32, two, three),
    ]


def tiles(ref, at, pitch):
    return [ref[pl.ds(m * pitch + at, G, stride=3 * pitch), :] for m in range(3)]


def products_kernel(
    a_ref, q_ref, g_ref, cols_ref, part_ref, dest_ref, pos_ref, dense_ref, h_ref, ht_ref, a_flat, q_flat, g_flat, nat, q_nat, q_tr, acc
):
    step = pl.program_id(0)
    fine = q_ref.shape[0]
    slots = a_ref.shape[1]
    n_part = acc.shape[0]
    width = a_ref.shape[2] // L

    @pl.when(step == 0)
    def _():
        for u in range(width):
            q_flat[u * fine : (u + 1) * fine, :] = q_ref[:, u * L : (u + 1) * L].astype(F32)
            g_flat[u * 8 : u * 8 + 3, :] = g_ref[:, u * L : (u + 1) * L]
        keep = lax.broadcasted_iota(jnp.int32, (B, L), 1) < B
        q_nat[:, B:, :] = jnp.zeros((fine, L - B, L), BF16)

        def one_q(i, _):
            rows = split_rows(tiles(q_flat, i, fine))
            for r in range(4):
                nat[pl.ds(r, G, stride=4), :] = rows[r]
            q_nat[i, :B, :] = jnp.where(keep, nat[...], 0.0).astype(BF16)
            permuted = jnp.concatenate(rows, axis=0)
            q_tr[i] = jnp.transpose(permuted)[:B].astype(BF16)
            return 0

        lax.fori_loop(0, fine, one_q, 0)

        mats = []
        for l in range(3):
            rows = split_rows(tiles(g_flat, l, 8))
            for r in range(4):
                nat[pl.ds(r, G, stride=4), :] = rows[r]
            mats.append(nat[...][:, :B])
        h = jnp.dot(mats[0], mats[1], precision=lax.Precision.HIGHEST, preferred_element_type=F32)
        h = jnp.dot(h, mats[2], precision=lax.Precision.HIGHEST, preferred_element_type=F32)
        h_ref[...] = jnp.zeros((L, L), F32)
        h_ref[:B, :B] = h
        nat[:, :B] = h
        ht_ref[...] = jnp.transpose(jnp.concatenate([nat[pl.ds(r, G, stride=4), :] for r in range(4)], axis=0))[:B]

        def clear(p, _):
            acc[p] = jnp.zeros((B, L), F32)
            return 0

        lax.fori_loop(0, n_part, clear, 0)

        def clear_dense(p, _):
            dense_ref[pl.ds(p * 128, 128), :] = jnp.zeros((128, L), F32)
            return 0

        lax.fori_loop(0, dense_ref.shape[0] // 128, clear_dense, 0)

    def one_row(rr, slot):
        i = step * ROWS + rr
        flat = a_flat.at[slot]
        for u in range(width):
            flat[u * slots : (u + 1) * slots, :] = a_ref[rr, :, u * L : (u + 1) * L].astype(F32)
        made = []
        for k in range(slots):
            block = jnp.concatenate(split_rows(tiles(flat, k, slots)), axis=0).astype(BF16)
            made.append(jnp.dot(block, q_nat[cols_ref[k, i]], preferred_element_type=F32).astype(BF16))
        term = jnp.dot(q_tr[i], jnp.concatenate(made, axis=1), preferred_element_type=F32)
        for k in range(slots):
            p = part_ref[k, i]
            acc[p] += term[:, k * L : (k + 1) * L]

    def pair(j, _):
        one_row(2 * j, 0)
        one_row(2 * j + 1, 1)
        return 0

    lax.fori_loop(0, ROWS // 2, pair, 0)

    @pl.when(step == pl.num_programs(0) - 1)
    def _():
        cell_rows = width * SC

        def one_part(p, _):
            place = pos_ref[p]
            base = (dest_ref[0, p] * RC + place // SC) * cell_rows + lax.rem(place, SC)
            flat = join_rows([acc[p, pl.ds(r, G, stride=4), :] for r in range(4)])
            for m in range(3):
                where = pl.ds(base + m * SC, G, stride=3 * SC)
                dense_ref[where, :] = dense_ref[where, :] + flat[m]
            return 0

        lax.fori_loop(0, n_part, one_part, 0)


def products(a_blocks, a_cols, q_blocks, part_of, part_dest, part_pos, g_level, n_inner):
    fine, slots, flat = a_blocks.shape
    n_part = part_pos.shape[0]
    width = flat // L
    smem = pl.BlockSpec(memory_space=pltpu.SMEM)
    vmem = pl.BlockSpec(memory_space=pltpu.VMEM)
    return pl.pallas_call(
        products_kernel,
        grid=(fine // ROWS,),
        out_shape=(
            jax.ShapeDtypeStruct((n_inner * RC * SC * width, L), F32),
            jax.ShapeDtypeStruct((L, L), F32),
            jax.ShapeDtypeStruct((B, B), F32),
        ),
        in_specs=[
            pl.BlockSpec((ROWS, slots, flat), lambda s: (s, 0, 0)),
            vmem,
            vmem,
            smem,
            smem,
            smem,
            smem,
        ],
        out_specs=(vmem, vmem, vmem),
        scratch_shapes=[
            pltpu.VMEM((2, width * slots, L), F32),
            pltpu.VMEM((width * fine, L), F32),
            pltpu.VMEM((width * 8, L), F32),
            pltpu.VMEM((B, L), F32),
            pltpu.VMEM((fine, L, L), BF16),
            pltpu.VMEM((fine, B, B), BF16),
            pltpu.VMEM((n_part, B, L), F32),
        ],
        compiler_params=pltpu.CompilerParams(dimension_semantics=("arbitrary",), vmem_limit_bytes=56 * 2**20),
        cost_estimate=pl.CostEstimate(flops=4 * fine * slots * B**3, bytes_accessed=a_blocks.size * 2, transcendentals=0),
    )(a_blocks, q_blocks, g_level, a_cols.T, part_of.T, part_dest.T, part_pos)


def merge_kernel(
    n_gx, pieces, depth, dense, h_ref, ht_ref, first_ref, last_ref,
    own, pair, right, left, half, give_half, other, slabs, mixed, parts, full, done, nat,
    local_sem, pair_send, pair_recv, right_send, right_recv, left_send, left_recv,
    core_send, core_recv, slab_send, slab_recv, part_send, part_recv, full_send, full_recv,
):
    gx = lax.axis_index("gx")
    gy = lax.axis_index("gy")
    n = own.shape[0]
    core, z = lax.rem(gy, 2), gy // 2
    owned = own.shape[1]
    cell_rows = owned // RC
    piece = owned // pieces
    peers = n_gx * 2
    share = cell_rows // peers
    rank = gx * 2 + lax.rem(z, 2)

    def remote(src, dst, send, recv, x, y):
        return pltpu.make_async_remote_copy(
            src_ref=src, dst_ref=dst, send_sem=send, recv_sem=recv, device_id=(x, y), device_id_type=pl.DeviceIdType.MESH
        )

    def peer(offset):
        other_rank = lax.rem(rank + offset, peers)
        return other_rank, other_rank // 2, (z // 2 * 2 + lax.rem(other_rank, 2)) * 2 + core

    barrier = pltpu.get_barrier_semaphore()

    def greet(x, y):
        pl.semaphore_signal(barrier, inc=1, device_id=(x, y), device_id_type=pl.DeviceIdType.MESH)

    partner = gy + 1 - 2 * core
    greet(gx, partner)

    for offset in range(1, n):
        greet(gx, 2 * lax.rem(z + offset, n) + core)
    for offset in range(1, n_gx):
        greet(lax.rem(gx + offset, n_gx), gy)
    for offset in range(1, peers):
        _, x, y = peer(offset)
        greet(x, y)

    def keep(d):
        return pltpu.make_async_copy(dense.at[2 * d + core], own.at[d], local_sem.at[d])

    def give(d):
        return remote(dense.at[2 * d + 1 - core], pair.at[d], pair_send.at[d], pair_recv.at[d], gx, partner)

    order = [d for t in range(n) for d in (n - 1 - t, t)][:n]
    for d in order:
        keep(d).start()
    pl.semaphore_wait(barrier, n + n_gx + peers - 2)
    for d in order:
        give(d).start()

    def go_right(d, c):
        rows = pl.ds(c * piece, piece)
        return remote(own.at[d, rows], right.at[d, rows], right_send.at[d, c], right_recv.at[d, c], gx, gy + 2)

    def go_left(d, c):
        rows = pl.ds(c * piece, piece)
        return remote(own.at[d, rows], left.at[d, rows], left_send.at[d, c], left_recv.at[d, c], gx, gy - 2)

    def arrive(d):
        keep(d).wait()
        give(d).wait_recv()
        own[d] = own[d] + pair[d]

    def step(s, _):
        t, c = s // pieces, lax.rem(s, pieces)
        rows = pl.ds(pl.multiple_of(c * piece, 8), piece)
        far, near = n - 1 - t, t
        back = s - depth
        back_t, back_c = jnp.maximum(back, 0) // pieces, lax.rem(jnp.maximum(back, 0), pieces)

        @pl.when((back >= 0) & (z < n - 1 - back_t))
        def _():
            go_right(n - 1 - back_t, back_c).wait_send()

        @pl.when((back >= 0) & (z > back_t))
        def _():
            go_left(back_t, back_c).wait_send()

        @pl.when(z < far)
        def _():
            @pl.when(z > 0)
            def _():
                go_right(far, c).wait_recv()
                own[far, rows] = own[far, rows] + right[far, rows]

            @pl.when((s > 0) | (z > 0))
            def _():
                go_right(far, c).start()

        @pl.when(z > near)
        def _():
            @pl.when(z < n - 1)
            def _():
                go_left(near, c).wait_recv()
                own[near, rows] = own[near, rows] + left[near, rows]

            @pl.when((s > 0) | (z < n - 1))
            def _():
                go_left(near, c).start()

        return 0

    groups = n // 2
    mine = pl.ds(pl.multiple_of(core * cell_rows, 8), cell_rows)
    theirs = pl.ds(pl.multiple_of((1 - core) * cell_rows, 8), cell_rows)
    swap = remote(give_half, other, core_send.at[0], core_recv.at[0], gx, partner)
    slab = cell_rows // n_gx
    here = pl.ds(pl.multiple_of(rank * share, 8), share)

    def group_sums():
        for g in range(groups):
            give_half[g] = own[2 * g, theirs] + own[2 * g + 1, theirs]
        swap.start()
        for g in range(groups):
            half[g] = own[2 * g, mine] + own[2 * g + 1, mine]

    def across(offset):
        to = lax.rem(gx + offset, n_gx)
        rows = pl.ds(pl.multiple_of(to * slab, 8), slab)
        at = n_gx - offset - 1
        return remote(half.at[:, rows], slabs.at[at], slab_send.at[offset - 1], slab_recv.at[at], to, gy)

    def crossed(offset):
        return remote(slabs.at[offset - 1], slabs.at[offset - 1], slab_send.at[offset - 1], slab_recv.at[offset - 1], gx, partner)

    def spread():
        swap.wait_recv()
        half[...] = half[...] + other[...]
        for offset in range(1, n_gx):
            across(offset).start()

    def along(offset):
        to = lax.rem(z + offset, n)
        rows = pl.ds(pl.multiple_of(lax.rem(to, 2) * share, 8), share)
        at = n - offset - 1
        return remote(mixed.at[to // 2, rows], parts.at[at], part_send.at[offset - 1], part_recv.at[at], gx, 2 * to + core)

    def went(offset):
        return remote(parts.at[offset - 1], parts.at[offset - 1], part_send.at[offset - 1], part_recv.at[offset - 1], gx, partner)

    def descend():
        total = half[:, pl.ds(pl.multiple_of(gx * slab, 8), slab)]
        for offset in range(1, n_gx):
            crossed(offset).wait_recv()
            total = total + slabs[offset - 1]
        mixed[...] = total
        for offset in range(1, n):
            along(offset).start()

    def gather(offset):
        _, x, y = peer(offset)
        return remote(full.at[here], full.at[here], full_send.at[offset - 1], full_recv.at[peers - offset - 1], x, y)

    def gathered(offset):
        source, x, y = peer(offset)
        rows = pl.ds(pl.multiple_of(source * share, 8), share)
        return remote(full.at[rows], full.at[rows], full_send.at[offset - 1], full_recv.at[offset - 1], x, y)

    def collect():
        total = mixed[z // 2, pl.ds(pl.multiple_of(lax.rem(z, 2) * share, 8), share)]
        for offset in range(1, n):
            went(offset).wait_recv()
            total = total + parts[offset - 1]
        full[here] = total
        for offset in range(1, peers):
            gather(offset).start()

    finish = remote(done.at[core], done.at[core], core_send.at[1], core_recv.at[1], gx, partner)
    finished = remote(done.at[1 - core], done.at[1 - core], core_send.at[1], core_recv.at[1], gx, partner)

    def project():
        for offset in range(1, peers):
            gathered(offset).wait_recv()
        blocks = jnp.concatenate([row for s in range(SC) for row in split_rows(tiles(full, s, SC))], axis=0)
        dot = functools.partial(jnp.dot, precision=lax.Precision.HIGHEST, preferred_element_type=F32)
        after = dot(blocks, h_ref[...])
        after = dot(ht_ref[...], jnp.concatenate([after[s * B : (s + 1) * B] for s in range(SC)], axis=1))
        for s in range(SC):
            nat[s] = after[:, s * L : (s + 1) * L]
            flat = join_rows([nat[s, pl.ds(r, G, stride=4), :] for r in range(4)])
            for m in range(3):
                done[core, pl.ds(m * SC + s, G, stride=3 * SC), :] = flat[m]
        finish.start()

    def write_last():
        finished.wait_recv()
        for u in range(cell_rows // SC):
            for r in range(RC):
                last_ref[r, :, u * L : (u + 1) * L] = done[r, u * SC : (u + 1) * SC, :]

    steps = (n - 1) * pieces
    arrive(n - 1)

    @pl.when(z == 0)
    def _():
        go_right(n - 1, 0).start()

    arrive(0)

    @pl.when(z == n - 1)
    def _():
        go_left(0, 0).start()

    for d in range(1, n - 1):
        arrive(d)
    at = 0
    for stage, stop in ((group_sums, 2), (spread, 4), (descend, 6), (collect, 8), (project, 10), (write_last, steps)):
        stage()
        lax.fori_loop(at, stop, step, 0)
        at = stop

    @pl.when(z < n - 1)
    def _():
        for c in range(pieces):
            go_left(z, c).wait_recv()
        own[z] = own[z] + left[z]

    @pl.when(z > 0)
    def _():
        for c in range(pieces):
            go_right(z, c).wait_recv()
        own[z] = own[z] + right[z]

    for u in range(cell_rows // SC):
        for r in range(RC):
            first_ref[r, :, u * L : (u + 1) * L] = own[z, r * cell_rows + u * SC : r * cell_rows + (u + 1) * SC, :]

    finish.wait_send()
    swap.wait_send()
    for offset in range(1, n_gx):
        across(offset).wait_send()
    for offset in range(1, n):
        along(offset).wait_send()
    for offset in range(1, peers):
        gather(offset).wait_send()
    for d in range(n):
        give(d).wait_send()
    for s in range(max(steps - depth, 0), steps):
        t, c = s // pieces, s % pieces

        @pl.when(z < n - 1 - t)
        def _():
            go_right(n - 1 - t, c).wait_send()

        @pl.when(z > t)
        def _():
            go_left(t, c).wait_send()


def merge(dense, h, ht, n_gx, n_inner, flat):
    pieces, depth = 4, 2
    n = n_inner // 2
    peers = n_gx * 2
    owned = dense.shape[0] // n_inner
    cell_rows = owned // RC
    vmem = pl.BlockSpec(memory_space=pltpu.VMEM)
    dma = pltpu.SemaphoreType.DMA
    out = jax.ShapeDtypeStruct((RC, SC, flat), F32)
    return pl.pallas_call(
        functools.partial(merge_kernel, n_gx, pieces, depth),
        out_shape=(out, out),
        in_specs=[pl.BlockSpec(memory_space=pl.ANY), vmem, vmem],
        out_specs=(vmem, vmem),
        scratch_shapes=[pltpu.VMEM((n, owned, L), F32)] * 4
        + [
            pltpu.VMEM((n // 2, cell_rows, L), F32),
            pltpu.VMEM((n // 2, cell_rows, L), F32),
            pltpu.VMEM((n // 2, cell_rows, L), F32),
            pltpu.VMEM((n_gx - 1, n // 2, cell_rows // n_gx, L), F32),
            pltpu.VMEM((n // 2, cell_rows // n_gx, L), F32),
            pltpu.VMEM((n - 1, cell_rows // peers, L), F32),
            pltpu.VMEM((cell_rows, L), F32),
            pltpu.VMEM((RC, cell_rows, L), F32),
            pltpu.VMEM((SC, B, L), F32),
            dma((n,)),
            dma((n,)),
            dma((n,)),
            dma((n, pieces)),
            dma((n, pieces)),
            dma((n, pieces)),
            dma((n, pieces)),
            dma((2,)),
            dma((2,)),
            dma((n_gx - 1,)),
            dma((n_gx - 1,)),
            dma((n - 1,)),
            dma((n - 1,)),
            dma((peers - 1,)),
            dma((peers - 1,)),
        ],
        compiler_params=pltpu.CompilerParams(collective_id=0, has_side_effects=True, vmem_limit_bytes=56 * 2**20),
        cost_estimate=pl.CostEstimate(flops=4 * RC * SC * B**3, bytes_accessed=dense.size * 4, transcendentals=0),
    )(dense.reshape(n_inner, owned, L), h, ht)


def local(a_blocks, a_cols, q_blocks, part_of, part_dest, part_pos, g_level):
    n_gx, n_inner = lax.axis_size("gx"), lax.axis_size("gy")
    dense, h, ht = products(a_blocks, a_cols, q_blocks, part_of, part_dest, part_pos, g_level, n_inner)
    return merge(dense, h, ht, n_gx, n_inner, a_blocks.shape[2])


def solution(mesh):
    placed = (
        P(("gx", "gy"), None, None),
        P(("gx", "gy"), None),
        P(("gx", "gy"), None),
        P(("gx", "gy"), None),
        P(("gx", "gy"), None),
        P(("gx", "gy")),
        P(),
    )
    return jax.shard_map(
        local,
        mesh=mesh,
        in_specs=placed,
        out_specs=(P(("gx", "gy"), None, None), P(("gx", "gy"), None, None)),
        check_vma=False,
    )
```

```python
import functools

import jax
import jax.numpy as jnp
from jax import lax
from jax.experimental import pallas as pl
from jax.experimental.pallas import tpu as pltpu
from jax.sharding import PartitionSpec as P

B = 96
L = 128
G = 24
RC = 2
SC = 8
ROWS = 8
F32 = jnp.float32
BF16 = jnp.bfloat16


def lanes():
    return lax.broadcasted_iota(jnp.int32, (G, L), 1)


def split_rows(t):
    lane = lanes()
    return [
        t[0],
        pltpu.roll(jnp.where(lane >= 96, t[0], t[1]), 32, 1),
        pltpu.roll(jnp.where(lane >= 64, t[1], t[2]), 64, 1),
        pltpu.roll(t[2], 96, 1),
    ]


def join_rows(c):
    lane = lanes()
    one = pltpu.roll(c[1], 96, 1)
    two = pltpu.roll(c[2], 64, 1)
    three = pltpu.roll(c[3], 32, 1)
    return [
        jnp.where(lane < 96, c[0], one),
        jnp.where(lane < 64, one, two),
        jnp.where(lane < 32, two, three),
    ]


def tiles(ref, at, pitch):
    return [ref[pl.ds(m * pitch + at, G, stride=3 * pitch), :] for m in range(3)]


def products_kernel(
    a_ref, q_ref, g_ref, cols_ref, part_ref, dest_ref, pos_ref, dense_ref, h_ref, ht_ref, a_flat, q_flat, g_flat, nat, q_nat, q_tr, acc
):
    step = pl.program_id(0)
    fine = q_ref.shape[0]
    slots = a_ref.shape[1]
    n_part = acc.shape[0]
    width = a_ref.shape[2] // L

    @pl.when(step == 0)
    def _():
        for u in range(width):
            q_flat[u * fine : (u + 1) * fine, :] = q_ref[:, u * L : (u + 1) * L].astype(F32)
            g_flat[u * 8 : u * 8 + 3, :] = g_ref[:, u * L : (u + 1) * L]
        keep = lax.broadcasted_iota(jnp.int32, (B, L), 1) < B
        q_nat[:, B:, :] = jnp.zeros((fine, L - B, L), BF16)

        def one_q(i, _):
            rows = split_rows(tiles(q_flat, i, fine))
            for r in range(4):
                nat[pl.ds(r, G, stride=4), :] = rows[r]
            q_nat[i, :B, :] = jnp.where(keep, nat[...], 0.0).astype(BF16)
            permuted = jnp.concatenate(rows, axis=0)
            q_tr[i] = jnp.transpose(permuted)[:B].astype(BF16)
            return 0

        lax.fori_loop(0, fine, one_q, 0)

        mats = []
        for l in range(3):
            rows = split_rows(tiles(g_flat, l, 8))
            for r in range(4):
                nat[pl.ds(r, G, stride=4), :] = rows[r]
            mats.append(nat[...][:, :B])
        h = jnp.dot(mats[0], mats[1], precision=lax.Precision.HIGHEST, preferred_element_type=F32)
        h = jnp.dot(h, mats[2], precision=lax.Precision.HIGHEST, preferred_element_type=F32)
        h_ref[...] = jnp.zeros((L, L), F32)
        h_ref[:B, :B] = h
        nat[:, :B] = h
        ht_ref[...] = jnp.transpose(jnp.concatenate([nat[pl.ds(r, G, stride=4), :] for r in range(4)], axis=0))[:B]

        def clear(p, _):
            acc[p] = jnp.zeros((B, L), F32)
            return 0

        lax.fori_loop(0, n_part, clear, 0)

        def clear_dense(p, _):
            dense_ref[pl.ds(p * 128, 128), :] = jnp.zeros((128, L), F32)
            return 0

        lax.fori_loop(0, dense_ref.shape[0] // 128, clear_dense, 0)

    def one_row(rr, slot):
        i = step * ROWS + rr
        flat = a_flat.at[slot]
        for u in range(width):
            flat[u * slots : (u + 1) * slots, :] = a_ref[rr, :, u * L : (u + 1) * L].astype(F32)
        made = []
        for k in range(slots):
            block = jnp.concatenate(split_rows(tiles(flat, k, slots)), axis=0).astype(BF16)
            made.append(jnp.dot(block, q_nat[cols_ref[k, i]], preferred_element_type=F32).astype(BF16))
        term = jnp.dot(q_tr[i], jnp.concatenate(made, axis=1), preferred_element_type=F32)
        for k in range(slots):
            p = part_ref[k, i]
            acc[p] += term[:, k * L : (k + 1) * L]

    def pair(j, _):
        one_row(2 * j, 0)
        one_row(2 * j + 1, 1)
        return 0

    lax.fori_loop(0, ROWS // 2, pair, 0)

    @pl.when(step == pl.num_programs(0) - 1)
    def _():
        cell_rows = width * SC

        def one_part(p, _):
            place = pos_ref[p]
            base = (dest_ref[0, p] * RC + place // SC) * cell_rows + lax.rem(place, SC)
            flat = join_rows([acc[p, pl.ds(r, G, stride=4), :] for r in range(4)])
            for m in range(3):
                where = pl.ds(base + m * SC, G, stride=3 * SC)
                dense_ref[where, :] = dense_ref[where, :] + flat[m]
            return 0

        lax.fori_loop(0, n_part, one_part, 0)


def products(a_blocks, a_cols, q_blocks, part_of, part_dest, part_pos, g_level, n_inner):
    fine, slots, flat = a_blocks.shape
    n_part = part_pos.shape[0]
    width = flat // L
    smem = pl.BlockSpec(memory_space=pltpu.SMEM)
    vmem = pl.BlockSpec(memory_space=pltpu.VMEM)
    return pl.pallas_call(
        products_kernel,
        grid=(fine // ROWS,),
        out_shape=(
            jax.ShapeDtypeStruct((n_inner * RC * SC * width, L), F32),
            jax.ShapeDtypeStruct((L, L), F32),
            jax.ShapeDtypeStruct((B, B), F32),
        ),
        in_specs=[
            pl.BlockSpec((ROWS, slots, flat), lambda s: (s, 0, 0)),
            vmem,
            vmem,
            smem,
            smem,
            smem,
            smem,
        ],
        out_specs=(vmem, vmem, vmem),
        scratch_shapes=[
            pltpu.VMEM((2, width * slots, L), F32),
            pltpu.VMEM((width * fine, L), F32),
            pltpu.VMEM((width * 8, L), F32),
            pltpu.VMEM((B, L), F32),
            pltpu.VMEM((fine, L, L), BF16),
            pltpu.VMEM((fine, B, B), BF16),
            pltpu.VMEM((n_part, B, L), F32),
        ],
        compiler_params=pltpu.CompilerParams(dimension_semantics=("arbitrary",), vmem_limit_bytes=56 * 2**20),
        cost_estimate=pl.CostEstimate(flops=4 * fine * slots * B**3, bytes_accessed=a_blocks.size * 2, transcendentals=0),
    )(a_blocks, q_blocks, g_level, a_cols.T, part_of.T, part_dest.T, part_pos)


def merge_kernel(
    n_gx, pieces, depth, dense, h_ref, ht_ref, first_ref, last_ref,
    own, pair, right, left, half, give_half, other, slabs, mixed, parts, full, done, nat,
    local_sem, pair_send, pair_recv, right_send, right_recv, left_send, left_recv,
    core_send, core_recv, slab_send, slab_recv, part_send, part_recv, full_send, full_recv,
):
    gx = lax.axis_index("gx")
    gy = lax.axis_index("gy")
    n = own.shape[0]
    core, z = lax.rem(gy, 2), gy // 2
    owned = own.shape[1]
    cell_rows = owned // RC
    piece = owned // pieces
    peers = n_gx * 2
    share = cell_rows // peers
    rank = gx * 2 + lax.rem(z, 2)

    def remote(src, dst, send, recv, x, y):
        return pltpu.make_async_remote_copy(
            src_ref=src, dst_ref=dst, send_sem=send, recv_sem=recv, device_id=(x, y), device_id_type=pl.DeviceIdType.MESH
        )

    barrier = pltpu.get_barrier_semaphore()

    def greet(x, y):
        pl.semaphore_signal(barrier, inc=1, device_id=(x, y), device_id_type=pl.DeviceIdType.MESH)

    partner = gy + 1 - 2 * core
    greet(gx, partner)

    for offset in range(1, n):
        greet(gx, 2 * lax.rem(z + offset, n) + core)
    for offset in range(1, n_gx):
        greet(lax.rem(gx + offset, n_gx), gy)

    def keep(d):
        return pltpu.make_async_copy(dense.at[2 * d + core], own.at[d], local_sem.at[d])

    def give(d):
        return remote(dense.at[2 * d + 1 - core], pair.at[d], pair_send.at[d], pair_recv.at[d], gx, partner)

    order = [d for t in range(n) for d in (n - 1 - t, t)][:n]
    for d in order:
        keep(d).start()
    pl.semaphore_wait(barrier, n + n_gx - 1)
    for d in order:
        give(d).start()

    def go_right(d, c):
        rows = pl.ds(c * piece, piece)
        return remote(own.at[d, rows], right.at[d, rows], right_send.at[d, c], right_recv.at[d, c], gx, gy + 2)

    def go_left(d, c):
        rows = pl.ds(c * piece, piece)
        return remote(own.at[d, rows], left.at[d, rows], left_send.at[d, c], left_recv.at[d, c], gx, gy - 2)

    def arrive(d):
        keep(d).wait()
        give(d).wait_recv()
        own[d] = own[d] + pair[d]

    def step(s, _):
        t, c = s // pieces, lax.rem(s, pieces)
        rows = pl.ds(pl.multiple_of(c * piece, 8), piece)
        far, near = n - 1 - t, t
        back = s - depth
        back_t, back_c = jnp.maximum(back, 0) // pieces, lax.rem(jnp.maximum(back, 0), pieces)

        @pl.when((back >= 0) & (z < n - 1 - back_t))
        def _():
            go_right(n - 1 - back_t, back_c).wait_send()

        @pl.when((back >= 0) & (z > back_t))
        def _():
            go_left(back_t, back_c).wait_send()

        @pl.when(z < far)
        def _():
            @pl.when(z > 0)
            def _():
                go_right(far, c).wait_recv()
                own[far, rows] = own[far, rows] + right[far, rows]

            @pl.when((s > 0) | (z > 0))
            def _():
                go_right(far, c).start()

        @pl.when(z > near)
        def _():
            @pl.when(z < n - 1)
            def _():
                go_left(near, c).wait_recv()
                own[near, rows] = own[near, rows] + left[near, rows]

            @pl.when((s > 0) | (z < n - 1))
            def _():
                go_left(near, c).start()

        return 0

    groups = n // 2
    mine = pl.ds(pl.multiple_of(core * cell_rows, 8), cell_rows)
    theirs = pl.ds(pl.multiple_of((1 - core) * cell_rows, 8), cell_rows)
    swap = remote(give_half, other, core_send.at[0], core_recv.at[0], gx, partner)
    slab = cell_rows // n_gx
    here = pl.ds(pl.multiple_of(rank * share, 8), share)

    def group_sums():
        for g in range(groups):
            give_half[g] = own[2 * g, theirs] + own[2 * g + 1, theirs]
        swap.start()
        for g in range(groups):
            half[g] = own[2 * g, mine] + own[2 * g + 1, mine]

    def across(offset):
        to = lax.rem(gx + offset, n_gx)
        rows = pl.ds(pl.multiple_of(to * slab, 8), slab)
        at = n_gx - offset - 1
        return remote(half.at[:, rows], slabs.at[at], slab_send.at[offset - 1], slab_recv.at[at], to, gy)

    def crossed(offset):
        return remote(slabs.at[offset - 1], slabs.at[offset - 1], slab_send.at[offset - 1], slab_recv.at[offset - 1], gx, partner)

    def spread():
        swap.wait_recv()
        half[...] = half[...] + other[...]
        for offset in range(1, n_gx):
            across(offset).start()

    def along(offset):
        to = lax.rem(z + offset, n)
        rows = pl.ds(pl.multiple_of(lax.rem(to, 2) * share, 8), share)
        at = n - offset - 1
        return remote(mixed.at[to // 2, rows], parts.at[at], part_send.at[offset - 1], part_recv.at[at], gx, 2 * to + core)

    def went(offset):
        return remote(parts.at[offset - 1], parts.at[offset - 1], part_send.at[offset - 1], part_recv.at[offset - 1], gx, partner)

    def descend():
        total = half[:, pl.ds(pl.multiple_of(gx * slab, 8), slab)]
        for offset in range(1, n_gx):
            crossed(offset).wait_recv()
            total = total + slabs[offset - 1]
        mixed[...] = total
        for offset in range(1, n):
            along(offset).start()

    twin = gy + 2 - 4 * lax.rem(z, 2)
    slab_rows = pl.ds(pl.multiple_of(gx * slab, 8), slab)
    pass_on = remote(full.at[here], full.at[here], core_send.at[2], core_recv.at[2], gx, twin)

    def gather(offset):
        to = lax.rem(gx + offset, n_gx)
        at = n_gx - offset - 1
        return remote(full.at[slab_rows], full.at[slab_rows], full_send.at[offset - 1], full_recv.at[at], to, gy)

    def gathered(offset):
        source = lax.rem(gx + offset, n_gx)
        rows = pl.ds(pl.multiple_of(source * slab, 8), slab)
        return remote(full.at[rows], full.at[rows], full_send.at[offset - 1], full_recv.at[offset - 1], source, gy)

    def collect():
        total = mixed[z // 2, pl.ds(pl.multiple_of(lax.rem(z, 2) * share, 8), share)]
        for offset in range(1, n):
            went(offset).wait_recv()
            total = total + parts[offset - 1]
        full[here] = total
        pass_on.start()

    def fan_out():
        other_rank = rank + 1 - 2 * lax.rem(rank, 2)
        rows = pl.ds(pl.multiple_of(other_rank * share, 8), share)
        remote(full.at[rows], full.at[rows], core_send.at[2], core_recv.at[2], gx, twin).wait_recv()
        for offset in range(1, n_gx):
            gather(offset).start()

    finish = remote(done.at[core], done.at[core], core_send.at[1], core_recv.at[1], gx, partner)
    finished = remote(done.at[1 - core], done.at[1 - core], core_send.at[1], core_recv.at[1], gx, partner)

    def project():
        for offset in range(1, n_gx):
            gathered(offset).wait_recv()
        blocks = jnp.concatenate([row for s in range(SC) for row in split_rows(tiles(full, s, SC))], axis=0)
        dot = functools.partial(jnp.dot, precision=lax.Precision.HIGHEST, preferred_element_type=F32)
        after = dot(blocks, h_ref[...])
        after = dot(ht_ref[...], jnp.concatenate([after[s * B : (s + 1) * B] for s in range(SC)], axis=1))
        for s in range(SC):
            nat[s] = after[:, s * L : (s + 1) * L]
            flat = join_rows([nat[s, pl.ds(r, G, stride=4), :] for r in range(4)])
            for m in range(3):
                done[core, pl.ds(m * SC + s, G, stride=3 * SC), :] = flat[m]
        finish.start()

    def write_last():
        finished.wait_recv()
        for u in range(cell_rows // SC):
            for r in range(RC):
                last_ref[r, :, u * L : (u + 1) * L] = done[r, u * SC : (u + 1) * SC, :]

    steps = (n - 1) * pieces
    arrive(n - 1)

    @pl.when(z == 0)
    def _():
        go_right(n - 1, 0).start()

    arrive(0)

    @pl.when(z == n - 1)
    def _():
        go_left(0, 0).start()

    for d in range(1, n - 1):
        arrive(d)
    edge = (z == 0) | (z == n - 1)
    busy = steps - pieces
    at = 0
    for stage, at_edge, between in (
        (group_sums, 2, 0),
        (spread, 4, 0),
        (descend, 6, 1),
        (collect, 7, 3),
        (fan_out, 9, busy),
        (project, 10, busy),
        (write_last, steps, steps),
    ):
        stage()
        stop = jnp.where(edge, at_edge, between)
        lax.fori_loop(at, stop, step, 0)
        at = stop

    @pl.when(z < n - 1)
    def _():
        for c in range(pieces):
            go_left(z, c).wait_recv()
        own[z] = own[z] + left[z]

    @pl.when(z > 0)
    def _():
        for c in range(pieces):
            go_right(z, c).wait_recv()
        own[z] = own[z] + right[z]

    for u in range(cell_rows // SC):
        for r in range(RC):
            first_ref[r, :, u * L : (u + 1) * L] = own[z, r * cell_rows + u * SC : r * cell_rows + (u + 1) * SC, :]

    finish.wait_send()
    swap.wait_send()
    for offset in range(1, n_gx):
        across(offset).wait_send()
    for offset in range(1, n):
        along(offset).wait_send()
    pass_on.wait_send()
    for offset in range(1, n_gx):
        gather(offset).wait_send()
    for d in range(n):
        give(d).wait_send()
    for s in range(max(steps - depth, 0), steps):
        t, c = s // pieces, s % pieces

        @pl.when(z < n - 1 - t)
        def _():
            go_right(n - 1 - t, c).wait_send()

        @pl.when(z > t)
        def _():
            go_left(t, c).wait_send()


def merge(dense, h, ht, n_gx, n_inner, flat):
    pieces, depth = 4, 4
    n = n_inner // 2
    peers = n_gx * 2
    owned = dense.shape[0] // n_inner
    cell_rows = owned // RC
    vmem = pl.BlockSpec(memory_space=pltpu.VMEM)
    dma = pltpu.SemaphoreType.DMA
    out = jax.ShapeDtypeStruct((RC, SC, flat), F32)
    return pl.pallas_call(
        functools.partial(merge_kernel, n_gx, pieces, depth),
        out_shape=(out, out),
        in_specs=[pl.BlockSpec(memory_space=pl.ANY), vmem, vmem],
        out_specs=(vmem, vmem),
        scratch_shapes=[pltpu.VMEM((n, owned, L), F32)] * 4
        + [
            pltpu.VMEM((n // 2, cell_rows, L), F32),
            pltpu.VMEM((n // 2, cell_rows, L), F32),
            pltpu.VMEM((n // 2, cell_rows, L), F32),
            pltpu.VMEM((n_gx - 1, n // 2, cell_rows // n_gx, L), F32),
            pltpu.VMEM((n // 2, cell_rows // n_gx, L), F32),
            pltpu.VMEM((n - 1, cell_rows // peers, L), F32),
            pltpu.VMEM((cell_rows, L), F32),
            pltpu.VMEM((RC, cell_rows, L), F32),
            pltpu.VMEM((SC, B, L), F32),
            dma((n,)),
            dma((n,)),
            dma((n,)),
            dma((n, pieces)),
            dma((n, pieces)),
            dma((n, pieces)),
            dma((n, pieces)),
            dma((3,)),
            dma((3,)),
            dma((n_gx - 1,)),
            dma((n_gx - 1,)),
            dma((n - 1,)),
            dma((n - 1,)),
            dma((n_gx - 1,)),
            dma((n_gx - 1,)),
        ],
        compiler_params=pltpu.CompilerParams(collective_id=0, has_side_effects=True, vmem_limit_bytes=56 * 2**20),
        cost_estimate=pl.CostEstimate(flops=4 * RC * SC * B**3, bytes_accessed=dense.size * 4, transcendentals=0),
    )(dense.reshape(n_inner, owned, L), h, ht)


def local(a_blocks, a_cols, q_blocks, part_of, part_dest, part_pos, g_level):
    n_gx, n_inner = lax.axis_size("gx"), lax.axis_size("gy")
    dense, h, ht = products(a_blocks, a_cols, q_blocks, part_of, part_dest, part_pos, g_level, n_inner)
    return merge(dense, h, ht, n_gx, n_inner, a_blocks.shape[2])


def solution(mesh):
    placed = (
        P(("gx", "gy"), None, None),
        P(("gx", "gy"), None),
        P(("gx", "gy"), None),
        P(("gx", "gy"), None),
        P(("gx", "gy"), None),
        P(("gx", "gy")),
        P(),
    )
    return jax.shard_map(
        local,
        mesh=mesh,
        in_specs=placed,
        out_specs=(P(("gx", "gy"), None, None), P(("gx", "gy"), None, None)),
        check_vma=False,
    )
```

```python
import functools

import jax
import jax.numpy as jnp
from jax import lax
from jax.experimental import pallas as pl
from jax.experimental.pallas import tpu as pltpu
from jax.sharding import PartitionSpec as P

B = 96
L = 128
G = 24
RC = 2
SC = 8
ROWS = 8
F32 = jnp.float32
BF16 = jnp.bfloat16


def lanes():
    return lax.broadcasted_iota(jnp.int32, (G, L), 1)


def split_rows(t):
    lane = lanes()
    return [
        t[0],
        pltpu.roll(jnp.where(lane >= 96, t[0], t[1]), 32, 1),
        pltpu.roll(jnp.where(lane >= 64, t[1], t[2]), 64, 1),
        pltpu.roll(t[2], 96, 1),
    ]


def join_rows(c):
    lane = lanes()
    one = pltpu.roll(c[1], 96, 1)
    two = pltpu.roll(c[2], 64, 1)
    three = pltpu.roll(c[3], 32, 1)
    return [
        jnp.where(lane < 96, c[0], one),
        jnp.where(lane < 64, one, two),
        jnp.where(lane < 32, two, three),
    ]


def tiles(ref, at, pitch):
    return [ref[pl.ds(m * pitch + at, G, stride=3 * pitch), :] for m in range(3)]


def products_kernel(
    a_ref, q_ref, g_ref, cols_ref, part_ref, dest_ref, pos_ref, dense_ref, h_ref, ht_ref, a_flat, q_flat, g_flat, nat, q_nat, q_tr, acc
):
    step = pl.program_id(0)
    fine = q_ref.shape[0]
    slots = a_ref.shape[1]
    n_part = acc.shape[0]
    width = a_ref.shape[2] // L

    @pl.when(step == 0)
    def _():
        for u in range(width):
            q_flat[u * fine : (u + 1) * fine, :] = q_ref[:, u * L : (u + 1) * L].astype(F32)
            g_flat[u * 8 : u * 8 + 3, :] = g_ref[:, u * L : (u + 1) * L]
        keep = lax.broadcasted_iota(jnp.int32, (B, L), 1) < B
        q_nat[:, B:, :] = jnp.zeros((fine, L - B, L), BF16)

        def one_q(i, _):
            rows = split_rows(tiles(q_flat, i, fine))
            for r in range(4):
                nat[pl.ds(r, G, stride=4), :] = rows[r]
            q_nat[i, :B, :] = jnp.where(keep, nat[...], 0.0).astype(BF16)
            permuted = jnp.concatenate(rows, axis=0)
            q_tr[i] = jnp.transpose(permuted)[:B].astype(BF16)
            return 0

        lax.fori_loop(0, fine, one_q, 0)

        mats = []
        for l in range(3):
            rows = split_rows(tiles(g_flat, l, 8))
            for r in range(4):
                nat[pl.ds(r, G, stride=4), :] = rows[r]
            mats.append(nat[...][:, :B])
        h = jnp.dot(mats[0], mats[1], precision=lax.Precision.HIGHEST, preferred_element_type=F32)
        h = jnp.dot(h, mats[2], precision=lax.Precision.HIGHEST, preferred_element_type=F32)
        h_ref[...] = jnp.zeros((L, L), F32)
        h_ref[:B, :B] = h
        nat[:, :B] = h
        ht_ref[...] = jnp.transpose(jnp.concatenate([nat[pl.ds(r, G, stride=4), :] for r in range(4)], axis=0))[:B]

        def clear(p, _):
            acc[p] = jnp.zeros((B, L), F32)
            return 0

        lax.fori_loop(0, n_part, clear, 0)

        def clear_dense(p, _):
            dense_ref[pl.ds(p * 128, 128), :] = jnp.zeros((128, L), F32)
            return 0

        lax.fori_loop(0, dense_ref.shape[0] // 128, clear_dense, 0)

    def one_row(rr, slot):
        i = step * ROWS + rr
        flat = a_flat.at[slot]
        for u in range(width):
            flat[u * slots : (u + 1) * slots, :] = a_ref[rr, :, u * L : (u + 1) * L].astype(F32)
        made = []
        for k in range(slots):
            block = jnp.concatenate(split_rows(tiles(flat, k, slots)), axis=0).astype(BF16)
            made.append(jnp.dot(block, q_nat[cols_ref[k, i]], preferred_element_type=F32).astype(BF16))
        term = jnp.dot(q_tr[i], jnp.concatenate(made, axis=1), preferred_element_type=F32)
        for k in range(slots):
            p = part_ref[k, i]
            acc[p] += term[:, k * L : (k + 1) * L]

    def pair(j, _):
        one_row(2 * j, 0)
        one_row(2 * j + 1, 1)
        return 0

    lax.fori_loop(0, ROWS // 2, pair, 0)

    @pl.when(step == pl.num_programs(0) - 1)
    def _():
        cell_rows = width * SC

        def one_part(p, _):
            place = pos_ref[p]
            base = (dest_ref[0, p] * RC + place // SC) * cell_rows + lax.rem(place, SC)
            flat = join_rows([acc[p, pl.ds(r, G, stride=4), :] for r in range(4)])
            for m in range(3):
                where = pl.ds(base + m * SC, G, stride=3 * SC)
                dense_ref[where, :] = dense_ref[where, :] + flat[m]
            return 0

        lax.fori_loop(0, n_part, one_part, 0)


def products(a_blocks, a_cols, q_blocks, part_of, part_dest, part_pos, g_level, n_inner):
    fine, slots, flat = a_blocks.shape
    n_part = part_pos.shape[0]
    width = flat // L
    smem = pl.BlockSpec(memory_space=pltpu.SMEM)
    vmem = pl.BlockSpec(memory_space=pltpu.VMEM)
    return pl.pallas_call(
        products_kernel,
        grid=(fine // ROWS,),
        out_shape=(
            jax.ShapeDtypeStruct((n_inner * RC * SC * width, L), F32),
            jax.ShapeDtypeStruct((L, L), F32),
            jax.ShapeDtypeStruct((B, B), F32),
        ),
        in_specs=[
            pl.BlockSpec((ROWS, slots, flat), lambda s: (s, 0, 0)),
            vmem,
            vmem,
            smem,
            smem,
            smem,
            smem,
        ],
        out_specs=(vmem, vmem, vmem),
        scratch_shapes=[
            pltpu.VMEM((2, width * slots, L), F32),
            pltpu.VMEM((width * fine, L), F32),
            pltpu.VMEM((width * 8, L), F32),
            pltpu.VMEM((B, L), F32),
            pltpu.VMEM((fine, L, L), BF16),
            pltpu.VMEM((fine, B, B), BF16),
            pltpu.VMEM((n_part, B, L), F32),
        ],
        compiler_params=pltpu.CompilerParams(dimension_semantics=("arbitrary",), vmem_limit_bytes=56 * 2**20),
        cost_estimate=pl.CostEstimate(flops=4 * fine * slots * B**3, bytes_accessed=a_blocks.size * 2, transcendentals=0),
    )(a_blocks, q_blocks, g_level, a_cols.T, part_of.T, part_dest.T, part_pos)


def merge_kernel(
    n_gx, pieces, depth, dense, h_ref, ht_ref, first_ref, last_ref,
    own, pair, right, left, half, give_half, other, slabs, mixed, parts, full, done, nat,
    local_sem, pair_send, pair_recv, right_send, right_recv, left_send, left_recv,
    core_send, core_recv, slab_send, slab_recv, part_send, part_recv, full_send, full_recv,
):
    gx = lax.axis_index("gx")
    gy = lax.axis_index("gy")
    n = own.shape[0]
    core, z = lax.rem(gy, 2), gy // 2
    owned = own.shape[1]
    cell_rows = owned // RC
    piece = owned // pieces
    peers = n_gx * 2
    share = cell_rows // peers
    rank = gx * 2 + lax.rem(z, 2)

    def remote(src, dst, send, recv, x, y):
        return pltpu.make_async_remote_copy(
            src_ref=src, dst_ref=dst, send_sem=send, recv_sem=recv, device_id=(x, y), device_id_type=pl.DeviceIdType.MESH
        )

    barrier = pltpu.get_barrier_semaphore()

    def greet(x, y):
        pl.semaphore_signal(barrier, inc=1, device_id=(x, y), device_id_type=pl.DeviceIdType.MESH)

    partner = gy + 1 - 2 * core
    greet(gx, partner)

    for offset in range(1, n):
        greet(gx, 2 * lax.rem(z + offset, n) + core)
    for offset in range(1, n_gx):
        greet(lax.rem(gx + offset, n_gx), gy)

    def keep(d):
        return pltpu.make_async_copy(dense.at[2 * d + core], own.at[d], local_sem.at[d])

    def give(d):
        return remote(dense.at[2 * d + 1 - core], pair.at[d], pair_send.at[d], pair_recv.at[d], gx, partner)

    order = [d for t in range(n) for d in (n - 1 - t, t)][:n]
    for d in order:
        keep(d).start()
    pl.semaphore_wait(barrier, n + n_gx - 1)
    for d in order:
        give(d).start()

    def go_right(d, c):
        rows = pl.ds(c * piece, piece)
        return remote(own.at[d, rows], right.at[d, rows], right_send.at[d, c], right_recv.at[d, c], gx, gy + 2)

    def go_left(d, c):
        rows = pl.ds(c * piece, piece)
        return remote(own.at[d, rows], left.at[d, rows], left_send.at[d, c], left_recv.at[d, c], gx, gy - 2)

    def end_right(c):
        rows = pl.ds(c * piece, piece)
        return remote(own.at[n - 1, rows], left.at[n - 1, rows], right_send.at[n - 1, c], left_recv.at[n - 1, c], gx, 2 * (n - 1) + core)

    def end_left(c):
        rows = pl.ds(c * piece, piece)
        return remote(own.at[0, rows], right.at[0, rows], left_send.at[0, c], right_recv.at[0, c], gx, core)

    def arrive(d):
        keep(d).wait()
        give(d).wait_recv()
        own[d] = own[d] + pair[d]

    def step(s, _):
        t, c = s // pieces, lax.rem(s, pieces)
        rows = pl.ds(pl.multiple_of(c * piece, 8), piece)
        far, near = n - 1 - t, t
        back = s - depth
        back_t, back_c = jnp.maximum(back, 0) // pieces, lax.rem(jnp.maximum(back, 0), pieces)

        @pl.when((back >= 0) & (z < n - 1 - back_t))
        def _():
            go_right(n - 1 - back_t, back_c).wait_send()

        @pl.when((back >= 0) & (z > back_t))
        def _():
            go_left(back_t, back_c).wait_send()

        @pl.when(z < far)
        def _():
            @pl.when((z > 1) | ((z > 0) & (t > 0)))
            def _():
                go_right(far, c).wait_recv()
                own[far, rows] = own[far, rows] + right[far, rows]

            @pl.when((t > 0) | (z > 0))
            def _():
                go_right(far, c).start()

            @pl.when((t == 0) & (s > 0) & (z == 0))
            def _():
                end_right(c).start()

        @pl.when(z > near)
        def _():
            @pl.when((z < n - 2) | ((z < n - 1) & (t > 0)))
            def _():
                go_left(near, c).wait_recv()
                own[near, rows] = own[near, rows] + left[near, rows]

            @pl.when((t > 0) | (z < n - 1))
            def _():
                go_left(near, c).start()

            @pl.when((t == 0) & (s > 0) & (z == n - 1))
            def _():
                end_left(c).start()

        return 0

    groups = n // 2
    mine = pl.ds(pl.multiple_of(core * cell_rows, 8), cell_rows)
    theirs = pl.ds(pl.multiple_of((1 - core) * cell_rows, 8), cell_rows)
    swap = remote(give_half, other, core_send.at[0], core_recv.at[0], gx, partner)
    slab = cell_rows // n_gx
    here = pl.ds(pl.multiple_of(rank * share, 8), share)

    def group_sums():
        for g in range(groups):
            give_half[g] = own[2 * g, theirs] + own[2 * g + 1, theirs]
        swap.start()
        for g in range(groups):
            half[g] = own[2 * g, mine] + own[2 * g + 1, mine]

    def across(offset):
        to = lax.rem(gx + offset, n_gx)
        rows = pl.ds(pl.multiple_of(to * slab, 8), slab)
        at = n_gx - offset - 1
        return remote(half.at[:, rows], slabs.at[at], slab_send.at[offset - 1], slab_recv.at[at], to, gy)

    def crossed(offset):
        return remote(slabs.at[offset - 1], slabs.at[offset - 1], slab_send.at[offset - 1], slab_recv.at[offset - 1], gx, partner)

    def spread():
        swap.wait_recv()
        half[...] = half[...] + other[...]
        for offset in range(1, n_gx):
            across(offset).start()

    def along(offset):
        to = lax.rem(z + offset, n)
        rows = pl.ds(pl.multiple_of(lax.rem(to, 2) * share, 8), share)
        at = n - offset - 1
        return remote(mixed.at[to // 2, rows], parts.at[at], part_send.at[offset - 1], part_recv.at[at], gx, 2 * to + core)

    def went(offset):
        return remote(parts.at[offset - 1], parts.at[offset - 1], part_send.at[offset - 1], part_recv.at[offset - 1], gx, partner)

    def descend():
        total = half[:, pl.ds(pl.multiple_of(gx * slab, 8), slab)]
        for offset in range(1, n_gx):
            crossed(offset).wait_recv()
            total = total + slabs[offset - 1]
        mixed[...] = total
        for offset in range(1, n):
            along(offset).start()

    twin = gy + 2 - 4 * lax.rem(z, 2)
    slab_rows = pl.ds(pl.multiple_of(gx * slab, 8), slab)
    pass_on = remote(full.at[here], full.at[here], core_send.at[2], core_recv.at[2], gx, twin)

    def gather(offset):
        to = lax.rem(gx + offset, n_gx)
        at = n_gx - offset - 1
        return remote(full.at[slab_rows], full.at[slab_rows], full_send.at[offset - 1], full_recv.at[at], to, gy)

    def gathered(offset):
        source = lax.rem(gx + offset, n_gx)
        rows = pl.ds(pl.multiple_of(source * slab, 8), slab)
        return remote(full.at[rows], full.at[rows], full_send.at[offset - 1], full_recv.at[offset - 1], source, gy)

    def collect():
        total = mixed[z // 2, pl.ds(pl.multiple_of(lax.rem(z, 2) * share, 8), share)]
        for offset in range(1, n):
            went(offset).wait_recv()
            total = total + parts[offset - 1]
        full[here] = total
        pass_on.start()

    def fan_out():
        other_rank = rank + 1 - 2 * lax.rem(rank, 2)
        rows = pl.ds(pl.multiple_of(other_rank * share, 8), share)
        remote(full.at[rows], full.at[rows], core_send.at[2], core_recv.at[2], gx, twin).wait_recv()
        for offset in range(1, n_gx):
            gather(offset).start()

    finish = remote(done.at[core], done.at[core], core_send.at[1], core_recv.at[1], gx, partner)
    finished = remote(done.at[1 - core], done.at[1 - core], core_send.at[1], core_recv.at[1], gx, partner)

    def project():
        for offset in range(1, n_gx):
            gathered(offset).wait_recv()
        blocks = jnp.concatenate([row for s in range(SC) for row in split_rows(tiles(full, s, SC))], axis=0)
        dot = functools.partial(jnp.dot, precision=lax.Precision.HIGHEST, preferred_element_type=F32)
        after = dot(blocks, h_ref[...])
        after = dot(ht_ref[...], jnp.concatenate([after[s * B : (s + 1) * B] for s in range(SC)], axis=1))
        for s in range(SC):
            nat[s] = after[:, s * L : (s + 1) * L]
            flat = join_rows([nat[s, pl.ds(r, G, stride=4), :] for r in range(4)])
            for m in range(3):
                done[core, pl.ds(m * SC + s, G, stride=3 * SC), :] = flat[m]
        finish.start()

    def write_last():
        finished.wait_recv()
        for u in range(cell_rows // SC):
            for r in range(RC):
                last_ref[r, :, u * L : (u + 1) * L] = done[r, u * SC : (u + 1) * SC, :]

    steps = (n - 1) * pieces
    arrive(n - 1)

    @pl.when(z == 0)
    def _():
        end_right(0).start()

    arrive(0)

    @pl.when(z == n - 1)
    def _():
        end_left(0).start()

    for d in range(1, n - 1):
        arrive(d)
    edge = (z == 0) | (z == n - 1)
    busy = steps - pieces
    at = 0
    for stage, at_edge, between in (
        (group_sums, 2, 0),
        (spread, 4, 0),
        (descend, 6, 1),
        (collect, 7, 3),
        (fan_out, 9, busy),
        (project, 10, busy),
        (write_last, steps, steps),
    ):
        stage()
        stop = jnp.where(edge, at_edge, between)
        lax.fori_loop(at, stop, step, 0)
        at = stop

    for c in range(pieces):
        go_left(z, c).wait_recv()
        go_right(z, c).wait_recv()
    own[z] = own[z] + left[z] + right[z]

    for u in range(cell_rows // SC):
        for r in range(RC):
            first_ref[r, :, u * L : (u + 1) * L] = own[z, r * cell_rows + u * SC : r * cell_rows + (u + 1) * SC, :]

    finish.wait_send()
    swap.wait_send()
    for offset in range(1, n_gx):
        across(offset).wait_send()
    for offset in range(1, n):
        along(offset).wait_send()
    pass_on.wait_send()
    for offset in range(1, n_gx):
        gather(offset).wait_send()
    for d in range(n):
        give(d).wait_send()
    for s in range(max(steps - depth, 0), steps):
        t, c = s // pieces, s % pieces

        @pl.when(z < n - 1 - t)
        def _():
            go_right(n - 1 - t, c).wait_send()

        @pl.when(z > t)
        def _():
            go_left(t, c).wait_send()


def merge(dense, h, ht, n_gx, n_inner, flat):
    pieces, depth = 4, 4
    n = n_inner // 2
    peers = n_gx * 2
    owned = dense.shape[0] // n_inner
    cell_rows = owned // RC
    vmem = pl.BlockSpec(memory_space=pltpu.VMEM)
    dma = pltpu.SemaphoreType.DMA
    out = jax.ShapeDtypeStruct((RC, SC, flat), F32)
    return pl.pallas_call(
        functools.partial(merge_kernel, n_gx, pieces, depth),
        out_shape=(out, out),
        in_specs=[pl.BlockSpec(memory_space=pl.ANY), vmem, vmem],
        out_specs=(vmem, vmem),
        scratch_shapes=[pltpu.VMEM((n, owned, L), F32)] * 4
        + [
            pltpu.VMEM((n // 2, cell_rows, L), F32),
            pltpu.VMEM((n // 2, cell_rows, L), F32),
            pltpu.VMEM((n // 2, cell_rows, L), F32),
            pltpu.VMEM((n_gx - 1, n // 2, cell_rows // n_gx, L), F32),
            pltpu.VMEM((n // 2, cell_rows // n_gx, L), F32),
            pltpu.VMEM((n - 1, cell_rows // peers, L), F32),
            pltpu.VMEM((cell_rows, L), F32),
            pltpu.VMEM((RC, cell_rows, L), F32),
            pltpu.VMEM((SC, B, L), F32),
            dma((n,)),
            dma((n,)),
            dma((n,)),
            dma((n, pieces)),
            dma((n, pieces)),
            dma((n, pieces)),
            dma((n, pieces)),
            dma((3,)),
            dma((3,)),
            dma((n_gx - 1,)),
            dma((n_gx - 1,)),
            dma((n - 1,)),
            dma((n - 1,)),
            dma((n_gx - 1,)),
            dma((n_gx - 1,)),
        ],
        compiler_params=pltpu.CompilerParams(collective_id=0, has_side_effects=True, vmem_limit_bytes=56 * 2**20),
        cost_estimate=pl.CostEstimate(flops=4 * RC * SC * B**3, bytes_accessed=dense.size * 4, transcendentals=0),
    )(dense.reshape(n_inner, owned, L), h, ht)


def local(a_blocks, a_cols, q_blocks, part_of, part_dest, part_pos, g_level):
    n_gx, n_inner = lax.axis_size("gx"), lax.axis_size("gy")
    dense, h, ht = products(a_blocks, a_cols, q_blocks, part_of, part_dest, part_pos, g_level, n_inner)
    return merge(dense, h, ht, n_gx, n_inner, a_blocks.shape[2])


def solution(mesh):
    placed = (
        P(("gx", "gy"), None, None),
        P(("gx", "gy"), None),
        P(("gx", "gy"), None),
        P(("gx", "gy"), None),
        P(("gx", "gy"), None),
        P(("gx", "gy")),
        P(),
    )
    return jax.shard_map(
        local,
        mesh=mesh,
        in_specs=placed,
        out_specs=(P(("gx", "gy"), None, None), P(("gx", "gy"), None, None)),
        check_vma=False,
    )
```

```python
import functools

import jax
import jax.numpy as jnp
from jax import lax
from jax.experimental import pallas as pl
from jax.experimental.pallas import tpu as pltpu
from jax.sharding import PartitionSpec as P

B = 96
L = 128
G = 24
RC = 2
SC = 8
ROWS = 8
UNROLL = 4
F32 = jnp.float32
BF16 = jnp.bfloat16


def lanes():
    return lax.broadcasted_iota(jnp.int32, (G, L), 1)


def split_rows(t):
    lane = lanes()
    return [
        t[0],
        pltpu.roll(jnp.where(lane >= 96, t[0], t[1]), 32, 1),
        pltpu.roll(jnp.where(lane >= 64, t[1], t[2]), 64, 1),
        pltpu.roll(t[2], 96, 1),
    ]


def join_rows(c):
    lane = lanes()
    one = pltpu.roll(c[1], 96, 1)
    two = pltpu.roll(c[2], 64, 1)
    three = pltpu.roll(c[3], 32, 1)
    return [
        jnp.where(lane < 96, c[0], one),
        jnp.where(lane < 64, one, two),
        jnp.where(lane < 32, two, three),
    ]


def tiles(ref, at, pitch):
    return [ref[pl.ds(m * pitch + at, G, stride=3 * pitch), :] for m in range(3)]


def products_kernel(
    a_ref, q_ref, g_ref, cols_ref, part_ref, dest_ref, pos_ref, dense_ref, h_ref, ht_ref, a_flat, q_flat, g_flat, nat, q_nat, q_tr, acc
):
    step = pl.program_id(0)
    fine = q_ref.shape[0]
    slots = a_ref.shape[1]
    n_part = acc.shape[0]
    width = a_ref.shape[2] // L

    @pl.when(step == 0)
    def _():
        for u in range(width):
            q_flat[u * fine : (u + 1) * fine, :] = q_ref[:, u * L : (u + 1) * L].astype(F32)
            g_flat[u * 8 : u * 8 + 3, :] = g_ref[:, u * L : (u + 1) * L]
        keep = lax.broadcasted_iota(jnp.int32, (B, L), 1) < B
        q_nat[:, B:, :] = jnp.zeros((fine, L - B, L), BF16)

        def some_q(j, _):
            for e in range(UNROLL):
                rows = split_rows(tiles(q_flat, UNROLL * j + e, fine))
                for r in range(4):
                    nat[e, pl.ds(r, G, stride=4), :] = rows[r]
                q_tr[UNROLL * j + e] = jnp.transpose(jnp.concatenate(rows, axis=0))[:B].astype(BF16)
            for e in range(UNROLL):
                q_nat[UNROLL * j + e, :B, :] = jnp.where(keep, nat[e], 0.0).astype(BF16)
            return 0

        lax.fori_loop(0, fine // UNROLL, some_q, 0)

        mats = []
        for l in range(3):
            rows = split_rows(tiles(g_flat, l, 8))
            for r in range(4):
                nat[0, pl.ds(r, G, stride=4), :] = rows[r]
            mats.append(nat[0][:, :B])
        h = jnp.dot(mats[0], mats[1], precision=lax.Precision.HIGHEST, preferred_element_type=F32)
        h = jnp.dot(h, mats[2], precision=lax.Precision.HIGHEST, preferred_element_type=F32)
        h_ref[...] = jnp.zeros((L, L), F32)
        h_ref[:B, :B] = h
        nat[0, :, :B] = h
        ht_ref[...] = jnp.transpose(jnp.concatenate([nat[0, pl.ds(r, G, stride=4), :] for r in range(4)], axis=0))[:B]

        def clear(p, _):
            acc[p] = jnp.zeros((B, L), F32)
            return 0

        lax.fori_loop(0, n_part, clear, 0)

        def clear_dense(p, _):
            dense_ref[pl.ds(p * 128, 128), :] = jnp.zeros((128, L), F32)
            return 0

        lax.fori_loop(0, dense_ref.shape[0] // 128, clear_dense, 0)

    def some_rows(j, _):
        for e in range(UNROLL):
            for u in range(width):
                a_flat[e, u * slots : (u + 1) * slots, :] = a_ref[UNROLL * j + e, :, u * L : (u + 1) * L].astype(F32)
        for e in range(UNROLL):
            i = step * ROWS + UNROLL * j + e
            made = []
            for k in range(slots):
                block = jnp.concatenate(split_rows(tiles(a_flat.at[e], k, slots)), axis=0).astype(BF16)
                made.append(jnp.dot(block, q_nat[cols_ref[k, i]], preferred_element_type=F32).astype(BF16))
            term = jnp.dot(q_tr[i], jnp.concatenate(made, axis=1), preferred_element_type=F32)
            for k in range(slots):
                p = part_ref[k, i]
                acc[p] += term[:, k * L : (k + 1) * L]
        return 0

    lax.fori_loop(0, ROWS // UNROLL, some_rows, 0)

    @pl.when(step == pl.num_programs(0) - 1)
    def _():
        cell_rows = width * SC

        def some_parts(j, _):
            flats = [join_rows([acc[UNROLL * j + e, pl.ds(r, G, stride=4), :] for r in range(4)]) for e in range(UNROLL)]
            for e in range(UNROLL):
                p = UNROLL * j + e
                place = pos_ref[p]
                base = (dest_ref[0, p] * RC + place // SC) * cell_rows + lax.rem(place, SC)
                for m in range(3):
                    where = pl.ds(base + m * SC, G, stride=3 * SC)
                    dense_ref[where, :] = dense_ref[where, :] + flats[e][m]
            return 0

        lax.fori_loop(0, n_part // UNROLL, some_parts, 0)


def products(a_blocks, a_cols, q_blocks, part_of, part_dest, part_pos, g_level, n_inner):
    fine, slots, flat = a_blocks.shape
    n_part = part_pos.shape[0]
    width = flat // L
    smem = pl.BlockSpec(memory_space=pltpu.SMEM)
    vmem = pl.BlockSpec(memory_space=pltpu.VMEM)
    return pl.pallas_call(
        products_kernel,
        grid=(fine // ROWS,),
        out_shape=(
            jax.ShapeDtypeStruct((n_inner * RC * SC * width, L), F32),
            jax.ShapeDtypeStruct((L, L), F32),
            jax.ShapeDtypeStruct((B, B), F32),
        ),
        in_specs=[
            pl.BlockSpec((ROWS, slots, flat), lambda s: (s, 0, 0)),
            vmem,
            vmem,
            smem,
            smem,
            smem,
            smem,
        ],
        out_specs=(vmem, vmem, vmem),
        scratch_shapes=[
            pltpu.VMEM((UNROLL, width * slots, L), F32),
            pltpu.VMEM((width * fine, L), F32),
            pltpu.VMEM((width * 8, L), F32),
            pltpu.VMEM((UNROLL, B, L), F32),
            pltpu.VMEM((fine, L, L), BF16),
            pltpu.VMEM((fine, B, B), BF16),
            pltpu.VMEM((n_part, B, L), F32),
        ],
        compiler_params=pltpu.CompilerParams(dimension_semantics=("arbitrary",), vmem_limit_bytes=56 * 2**20),
        cost_estimate=pl.CostEstimate(flops=4 * fine * slots * B**3, bytes_accessed=a_blocks.size * 2, transcendentals=0),
    )(a_blocks, q_blocks, g_level, a_cols.T, part_of.T, part_dest.T, part_pos)


def merge_kernel(
    n_gx, pieces, depth, dense, h_ref, ht_ref, first_ref, last_ref,
    own, pair, right, left, half, give_half, other, slabs, mixed, parts, full, done, nat,
    local_sem, pair_send, pair_recv, right_send, right_recv, left_send, left_recv,
    core_send, core_recv, slab_send, slab_recv, part_send, part_recv, full_send, full_recv,
):
    gx = lax.axis_index("gx")
    gy = lax.axis_index("gy")
    n = own.shape[0]
    core, z = lax.rem(gy, 2), gy // 2
    owned = own.shape[1]
    cell_rows = owned // RC
    piece = owned // pieces
    peers = n_gx * 2
    share = cell_rows // peers
    rank = gx * 2 + lax.rem(z, 2)

    def remote(src, dst, send, recv, x, y):
        return pltpu.make_async_remote_copy(
            src_ref=src, dst_ref=dst, send_sem=send, recv_sem=recv, device_id=(x, y), device_id_type=pl.DeviceIdType.MESH
        )

    barrier = pltpu.get_barrier_semaphore()

    def greet(x, y):
        pl.semaphore_signal(barrier, inc=1, device_id=(x, y), device_id_type=pl.DeviceIdType.MESH)

    partner = gy + 1 - 2 * core
    greet(gx, partner)

    for offset in range(1, n):
        greet(gx, 2 * lax.rem(z + offset, n) + core)
    for offset in range(1, n_gx):
        greet(lax.rem(gx + offset, n_gx), gy)

    def keep(d):
        return pltpu.make_async_copy(dense.at[2 * d + core], own.at[d], local_sem.at[d])

    def give(d):
        return remote(dense.at[2 * d + 1 - core], pair.at[d], pair_send.at[d], pair_recv.at[d], gx, partner)

    order = [d for t in range(n) for d in (n - 1 - t, t)][:n]
    for d in order:
        keep(d).start()
    pl.semaphore_wait(barrier, n + n_gx - 1)
    for d in order:
        give(d).start()

    def go_right(d, c):
        rows = pl.ds(c * piece, piece)
        return remote(own.at[d, rows], right.at[d, rows], right_send.at[d, c], right_recv.at[d, c], gx, gy + 2)

    def go_left(d, c):
        rows = pl.ds(c * piece, piece)
        return remote(own.at[d, rows], left.at[d, rows], left_send.at[d, c], left_recv.at[d, c], gx, gy - 2)

    def arrive(d):
        keep(d).wait()
        give(d).wait_recv()
        own[d] = own[d] + pair[d]

    def step(s, _):
        t, c = s // pieces, lax.rem(s, pieces)
        rows = pl.ds(pl.multiple_of(c * piece, 8), piece)
        far, near = n - 1 - t, t
        back = s - depth
        back_t, back_c = jnp.maximum(back, 0) // pieces, lax.rem(jnp.maximum(back, 0), pieces)

        @pl.when((back >= 0) & (z < n - 1 - back_t))
        def _():
            go_right(n - 1 - back_t, back_c).wait_send()

        @pl.when((back >= 0) & (z > back_t))
        def _():
            go_left(back_t, back_c).wait_send()

        @pl.when(z < far)
        def _():
            @pl.when(z > 0)
            def _():
                go_right(far, c).wait_recv()
                own[far, rows] = own[far, rows] + right[far, rows]

            @pl.when((s > 0) | (z > 0))
            def _():
                go_right(far, c).start()

        @pl.when(z > near)
        def _():
            @pl.when(z < n - 1)
            def _():
                go_left(near, c).wait_recv()
                own[near, rows] = own[near, rows] + left[near, rows]

            @pl.when((s > 0) | (z < n - 1))
            def _():
                go_left(near, c).start()

        return 0

    groups = n // 2
    mine = pl.ds(pl.multiple_of(core * cell_rows, 8), cell_rows)
    theirs = pl.ds(pl.multiple_of((1 - core) * cell_rows, 8), cell_rows)
    swap = remote(give_half, other, core_send.at[0], core_recv.at[0], gx, partner)
    slab = cell_rows // n_gx
    here = pl.ds(pl.multiple_of(rank * share, 8), share)

    def group_sums():
        for g in range(groups):
            give_half[g] = own[2 * g, theirs] + own[2 * g + 1, theirs]
        swap.start()
        for g in range(groups):
            half[g] = own[2 * g, mine] + own[2 * g + 1, mine]

    def across(offset):
        to = lax.rem(gx + offset, n_gx)
        rows = pl.ds(pl.multiple_of(to * slab, 8), slab)
        at = n_gx - offset - 1
        return remote(half.at[:, rows], slabs.at[at], slab_send.at[offset - 1], slab_recv.at[at], to, gy)

    def crossed(offset):
        return remote(slabs.at[offset - 1], slabs.at[offset - 1], slab_send.at[offset - 1], slab_recv.at[offset - 1], gx, partner)

    def spread():
        swap.wait_recv()
        half[...] = half[...] + other[...]
        for offset in range(1, n_gx):
            across(offset).start()

    def along(offset):
        to = lax.rem(z + offset, n)
        rows = pl.ds(pl.multiple_of(lax.rem(to, 2) * share, 8), share)
        at = n - offset - 1
        return remote(mixed.at[to // 2, rows], parts.at[at], part_send.at[offset - 1], part_recv.at[at], gx, 2 * to + core)

    def went(offset):
        return remote(parts.at[offset - 1], parts.at[offset - 1], part_send.at[offset - 1], part_recv.at[offset - 1], gx, partner)

    def descend():
        total = half[:, pl.ds(pl.multiple_of(gx * slab, 8), slab)]
        for offset in range(1, n_gx):
            crossed(offset).wait_recv()
            total = total + slabs[offset - 1]
        mixed[...] = total
        for offset in range(1, n):
            along(offset).start()

    twin = gy + 2 - 4 * lax.rem(z, 2)
    slab_rows = pl.ds(pl.multiple_of(gx * slab, 8), slab)
    pass_on = remote(full.at[here], full.at[here], core_send.at[2], core_recv.at[2], gx, twin)

    def gather(offset):
        to = lax.rem(gx + offset, n_gx)
        at = n_gx - offset - 1
        return remote(full.at[slab_rows], full.at[slab_rows], full_send.at[offset - 1], full_recv.at[at], to, gy)

    def gathered(offset):
        source = lax.rem(gx + offset, n_gx)
        rows = pl.ds(pl.multiple_of(source * slab, 8), slab)
        return remote(full.at[rows], full.at[rows], full_send.at[offset - 1], full_recv.at[offset - 1], source, gy)

    def collect():
        total = mixed[z // 2, pl.ds(pl.multiple_of(lax.rem(z, 2) * share, 8), share)]
        for offset in range(1, n):
            went(offset).wait_recv()
            total = total + parts[offset - 1]
        full[here] = total
        pass_on.start()

    def fan_out():
        other_rank = rank + 1 - 2 * lax.rem(rank, 2)
        rows = pl.ds(pl.multiple_of(other_rank * share, 8), share)
        remote(full.at[rows], full.at[rows], core_send.at[2], core_recv.at[2], gx, twin).wait_recv()
        for offset in range(1, n_gx):
            gather(offset).start()

    finish = remote(done.at[core], done.at[core], core_send.at[1], core_recv.at[1], gx, partner)
    finished = remote(done.at[1 - core], done.at[1 - core], core_send.at[1], core_recv.at[1], gx, partner)

    def project():
        for offset in range(1, n_gx):
            gathered(offset).wait_recv()
        blocks = jnp.concatenate([row for s in range(SC) for row in split_rows(tiles(full, s, SC))], axis=0)
        dot = functools.partial(jnp.dot, precision=lax.Precision.HIGHEST, preferred_element_type=F32)
        after = dot(blocks, h_ref[...])
        after = dot(ht_ref[...], jnp.concatenate([after[s * B : (s + 1) * B] for s in range(SC)], axis=1))
        for s in range(SC):
            nat[s] = after[:, s * L : (s + 1) * L]
            flat = join_rows([nat[s, pl.ds(r, G, stride=4), :] for r in range(4)])
            for m in range(3):
                done[core, pl.ds(m * SC + s, G, stride=3 * SC), :] = flat[m]
        finish.start()

    def write_last():
        finished.wait_recv()
        for u in range(cell_rows // SC):
            for r in range(RC):
                last_ref[r, :, u * L : (u + 1) * L] = done[r, u * SC : (u + 1) * SC, :]

    steps = (n - 1) * pieces
    arrive(n - 1)

    @pl.when(z == 0)
    def _():
        go_right(n - 1, 0).start()

    arrive(0)

    @pl.when(z == n - 1)
    def _():
        go_left(0, 0).start()

    for d in range(1, n - 1):
        arrive(d)
    edge = (z == 0) | (z == n - 1)
    busy = steps - pieces
    at = 0
    for stage, at_edge, between in (
        (group_sums, 2, 0),
        (spread, 4, 0),
        (descend, 6, 1),
        (collect, 7, 3),
        (fan_out, 9, busy),
        (project, 10, busy),
        (write_last, steps, steps),
    ):
        stage()
        stop = jnp.where(edge, at_edge, between)
        lax.fori_loop(at, stop, step, 0)
        at = stop

    @pl.when(z < n - 1)
    def _():
        for c in range(pieces):
            go_left(z, c).wait_recv()
        own[z] = own[z] + left[z]

    @pl.when(z > 0)
    def _():
        for c in range(pieces):
            go_right(z, c).wait_recv()
        own[z] = own[z] + right[z]

    for u in range(cell_rows // SC):
        for r in range(RC):
            first_ref[r, :, u * L : (u + 1) * L] = own[z, r * cell_rows + u * SC : r * cell_rows + (u + 1) * SC, :]

    finish.wait_send()
    swap.wait_send()
    for offset in range(1, n_gx):
        across(offset).wait_send()
    for offset in range(1, n):
        along(offset).wait_send()
    pass_on.wait_send()
    for offset in range(1, n_gx):
        gather(offset).wait_send()
    for d in range(n):
        give(d).wait_send()
    for s in range(max(steps - depth, 0), steps):
        t, c = s // pieces, s % pieces

        @pl.when(z < n - 1 - t)
        def _():
            go_right(n - 1 - t, c).wait_send()

        @pl.when(z > t)
        def _():
            go_left(t, c).wait_send()


def merge(dense, h, ht, n_gx, n_inner, flat):
    pieces, depth = 4, 4
    n = n_inner // 2
    peers = n_gx * 2
    owned = dense.shape[0] // n_inner
    cell_rows = owned // RC
    vmem = pl.BlockSpec(memory_space=pltpu.VMEM)
    dma = pltpu.SemaphoreType.DMA
    out = jax.ShapeDtypeStruct((RC, SC, flat), F32)
    return pl.pallas_call(
        functools.partial(merge_kernel, n_gx, pieces, depth),
        out_shape=(out, out),
        in_specs=[pl.BlockSpec(memory_space=pl.ANY), vmem, vmem],
        out_specs=(vmem, vmem),
        scratch_shapes=[pltpu.VMEM((n, owned, L), F32)] * 4
        + [
            pltpu.VMEM((n // 2, cell_rows, L), F32),
            pltpu.VMEM((n // 2, cell_rows, L), F32),
            pltpu.VMEM((n // 2, cell_rows, L), F32),
            pltpu.VMEM((n_gx - 1, n // 2, cell_rows // n_gx, L), F32),
            pltpu.VMEM((n // 2, cell_rows // n_gx, L), F32),
            pltpu.VMEM((n - 1, cell_rows // peers, L), F32),
            pltpu.VMEM((cell_rows, L), F32),
            pltpu.VMEM((RC, cell_rows, L), F32),
            pltpu.VMEM((SC, B, L), F32),
            dma((n,)),
            dma((n,)),
            dma((n,)),
            dma((n, pieces)),
            dma((n, pieces)),
            dma((n, pieces)),
            dma((n, pieces)),
            dma((3,)),
            dma((3,)),
            dma((n_gx - 1,)),
            dma((n_gx - 1,)),
            dma((n - 1,)),
            dma((n - 1,)),
            dma((n_gx - 1,)),
            dma((n_gx - 1,)),
        ],
        compiler_params=pltpu.CompilerParams(collective_id=0, has_side_effects=True, vmem_limit_bytes=56 * 2**20),
        cost_estimate=pl.CostEstimate(flops=4 * RC * SC * B**3, bytes_accessed=dense.size * 4, transcendentals=0),
    )(dense.reshape(n_inner, owned, L), h, ht)


def hand_over_kernel(first_in, last_in, first_ref, last_ref, sems):
    copies = []
    for r in range(RC):
        copies.append(pltpu.make_async_copy(first_in.at[r], first_ref.at[r], sems.at[0, r]))
        copies.append(pltpu.make_async_copy(last_in.at[r], last_ref.at[r], sems.at[1, r]))
    for copy in copies:
        copy.start()
    for copy in copies:
        copy.wait()


def hand_over(first, last):
    anywhere = pl.BlockSpec(memory_space=pl.ANY)
    return pl.pallas_call(
        hand_over_kernel,
        out_shape=(jax.ShapeDtypeStruct(first.shape, F32), jax.ShapeDtypeStruct(last.shape, F32)),
        in_specs=[anywhere, anywhere],
        out_specs=(anywhere, anywhere),
        scratch_shapes=[pltpu.SemaphoreType.DMA((2, RC))],
        compiler_params=pltpu.CompilerParams(vmem_limit_bytes=56 * 2**20),
    )(first, last)


def local(a_blocks, a_cols, q_blocks, part_of, part_dest, part_pos, g_level):
    n_gx, n_inner = lax.axis_size("gx"), lax.axis_size("gy")
    dense, h, ht = products(a_blocks, a_cols, q_blocks, part_of, part_dest, part_pos, g_level, n_inner)
    return hand_over(*merge(dense, h, ht, n_gx, n_inner, a_blocks.shape[2]))


def solution(mesh):
    placed = (
        P(("gx", "gy"), None, None),
        P(("gx", "gy"), None),
        P(("gx", "gy"), None),
        P(("gx", "gy"), None),
        P(("gx", "gy"), None),
        P(("gx", "gy")),
        P(),
    )
    return jax.shard_map(
        local,
        mesh=mesh,
        in_specs=placed,
        out_specs=(P(("gx", "gy"), None, None), P(("gx", "gy"), None, None)),
        check_vma=False,
    )
```

```python
import functools

import jax
import jax.numpy as jnp
from jax import lax
from jax.experimental import pallas as pl
from jax.experimental.pallas import tpu as pltpu
from jax.sharding import PartitionSpec as P

B = 96
L = 128
G = 24
RC = 2
SC = 8
ROWS = 8
UNROLL = 8
F32 = jnp.float32
BF16 = jnp.bfloat16


def lanes():
    return lax.broadcasted_iota(jnp.int32, (G, L), 1)


def split_rows(t):
    lane = lanes()
    return [
        t[0],
        pltpu.roll(jnp.where(lane >= 96, t[0], t[1]), 32, 1),
        pltpu.roll(jnp.where(lane >= 64, t[1], t[2]), 64, 1),
        pltpu.roll(t[2], 96, 1),
    ]


def join_rows(c):
    lane = lanes()
    one = pltpu.roll(c[1], 96, 1)
    two = pltpu.roll(c[2], 64, 1)
    three = pltpu.roll(c[3], 32, 1)
    return [
        jnp.where(lane < 96, c[0], one),
        jnp.where(lane < 64, one, two),
        jnp.where(lane < 32, two, three),
    ]


def tiles(ref, at, pitch):
    return [ref[pl.ds(m * pitch + at, G, stride=3 * pitch), :] for m in range(3)]


def products_kernel(
    a_ref, q_ref, g_ref, cols_ref, part_ref, dest_ref, pos_ref, dense_ref, h_ref, ht_ref, a_flat, q_flat, g_flat, nat, q_nat, q_tr, acc
):
    step = pl.program_id(0)
    fine = q_ref.shape[0]
    slots = a_ref.shape[1]
    n_part = acc.shape[0]
    width = a_ref.shape[2] // L

    @pl.when(step == 0)
    def _():
        for u in range(width):
            q_flat[u * fine : (u + 1) * fine, :] = q_ref[:, u * L : (u + 1) * L].astype(F32)
            g_flat[u * 8 : u * 8 + 3, :] = g_ref[:, u * L : (u + 1) * L]
        keep = lax.broadcasted_iota(jnp.int32, (B, L), 1) < B
        q_nat[:, B:, :] = jnp.zeros((fine, L - B, L), BF16)

        def some_q(j, _):
            for e in range(UNROLL):
                rows = split_rows(tiles(q_flat, UNROLL * j + e, fine))
                for r in range(4):
                    nat[e, pl.ds(r, G, stride=4), :] = rows[r]
                q_tr[UNROLL * j + e] = jnp.transpose(jnp.concatenate(rows, axis=0))[:B].astype(BF16)
            for e in range(UNROLL):
                q_nat[UNROLL * j + e, :B, :] = jnp.where(keep, nat[e], 0.0).astype(BF16)
            return 0

        lax.fori_loop(0, fine // UNROLL, some_q, 0)

        mats = []
        for l in range(3):
            rows = split_rows(tiles(g_flat, l, 8))
            for r in range(4):
                nat[0, pl.ds(r, G, stride=4), :] = rows[r]
            mats.append(nat[0][:, :B])
        h = jnp.dot(mats[0], mats[1], precision=lax.Precision.HIGHEST, preferred_element_type=F32)
        h = jnp.dot(h, mats[2], precision=lax.Precision.HIGHEST, preferred_element_type=F32)
        h_ref[...] = jnp.zeros((L, L), F32)
        h_ref[:B, :B] = h
        nat[0, :, :B] = h
        ht_ref[...] = jnp.transpose(jnp.concatenate([nat[0, pl.ds(r, G, stride=4), :] for r in range(4)], axis=0))[:B]

        def clear(p, _):
            acc[p] = jnp.zeros((B, L), F32)
            return 0

        lax.fori_loop(0, n_part, clear, 0)

        def clear_dense(p, _):
            dense_ref[pl.ds(p * 128, 128), :] = jnp.zeros((128, L), F32)
            return 0

        lax.fori_loop(0, dense_ref.shape[0] // 128, clear_dense, 0)

    def some_rows(j, _):
        for e in range(UNROLL):
            for u in range(width):
                a_flat[e, u * slots : (u + 1) * slots, :] = a_ref[UNROLL * j + e, :, u * L : (u + 1) * L].astype(F32)
        for e in range(UNROLL):
            i = step * ROWS + UNROLL * j + e
            made = []
            for k in range(slots):
                block = jnp.concatenate(split_rows(tiles(a_flat.at[e], k, slots)), axis=0).astype(BF16)
                made.append(jnp.dot(block, q_nat[cols_ref[k, i]], preferred_element_type=F32).astype(BF16))
            term = jnp.dot(q_tr[i], jnp.concatenate(made, axis=1), preferred_element_type=F32)
            for k in range(slots):
                p = part_ref[k, i]
                acc[p] += term[:, k * L : (k + 1) * L]
        return 0

    lax.fori_loop(0, ROWS // UNROLL, some_rows, 0)

    @pl.when(step == pl.num_programs(0) - 1)
    def _():
        cell_rows = width * SC

        def some_parts(j, _):
            flats = [join_rows([acc[UNROLL * j + e, pl.ds(r, G, stride=4), :] for r in range(4)]) for e in range(UNROLL)]
            for e in range(UNROLL):
                p = UNROLL * j + e
                place = pos_ref[p]
                base = (dest_ref[0, p] * RC + place // SC) * cell_rows + lax.rem(place, SC)
                for m in range(3):
                    where = pl.ds(base + m * SC, G, stride=3 * SC)
                    dense_ref[where, :] = dense_ref[where, :] + flats[e][m]
            return 0

        lax.fori_loop(0, n_part // UNROLL, some_parts, 0)


def products(a_blocks, a_cols, q_blocks, part_of, part_dest, part_pos, g_level, n_inner):
    fine, slots, flat = a_blocks.shape
    n_part = part_pos.shape[0]
    width = flat // L
    smem = pl.BlockSpec(memory_space=pltpu.SMEM)
    vmem = pl.BlockSpec(memory_space=pltpu.VMEM)
    return pl.pallas_call(
        products_kernel,
        grid=(fine // ROWS,),
        out_shape=(
            jax.ShapeDtypeStruct((n_inner * RC * SC * width, L), F32),
            jax.ShapeDtypeStruct((L, L), F32),
            jax.ShapeDtypeStruct((B, B), F32),
        ),
        in_specs=[
            pl.BlockSpec((ROWS, slots, flat), lambda s: (s, 0, 0)),
            vmem,
            vmem,
            smem,
            smem,
            smem,
            smem,
        ],
        out_specs=(vmem, vmem, vmem),
        scratch_shapes=[
            pltpu.VMEM((UNROLL, width * slots, L), F32),
            pltpu.VMEM((width * fine, L), F32),
            pltpu.VMEM((width * 8, L), F32),
            pltpu.VMEM((UNROLL, B, L), F32),
            pltpu.VMEM((fine, L, L), BF16),
            pltpu.VMEM((fine, B, B), BF16),
            pltpu.VMEM((n_part, B, L), F32),
        ],
        compiler_params=pltpu.CompilerParams(dimension_semantics=("arbitrary",), vmem_limit_bytes=56 * 2**20),
        cost_estimate=pl.CostEstimate(flops=4 * fine * slots * B**3, bytes_accessed=a_blocks.size * 2, transcendentals=0),
    )(a_blocks, q_blocks, g_level, a_cols.T, part_of.T, part_dest.T, part_pos)


def merge_kernel(
    n_gx, pieces, depth, dense, h_ref, ht_ref, first_ref, last_ref,
    own, pair, right, left, half, give_half, other, slabs, mixed, parts, full, done, nat,
    local_sem, pair_send, pair_recv, right_send, right_recv, left_send, left_recv,
    core_send, core_recv, slab_send, slab_recv, part_send, part_recv, full_send, full_recv,
):
    gx = lax.axis_index("gx")
    gy = lax.axis_index("gy")
    n = own.shape[0]
    core, z = lax.rem(gy, 2), gy // 2
    owned = own.shape[1]
    cell_rows = owned // RC
    piece = owned // pieces
    peers = n_gx * 2
    share = cell_rows // peers
    rank = gx * 2 + lax.rem(z, 2)

    def remote(src, dst, send, recv, x, y):
        return pltpu.make_async_remote_copy(
            src_ref=src, dst_ref=dst, send_sem=send, recv_sem=recv, device_id=(x, y), device_id_type=pl.DeviceIdType.MESH
        )

    barrier = pltpu.get_barrier_semaphore()

    def greet(x, y):
        pl.semaphore_signal(barrier, inc=1, device_id=(x, y), device_id_type=pl.DeviceIdType.MESH)

    partner = gy + 1 - 2 * core
    greet(gx, partner)

    for offset in range(1, n):
        greet(gx, 2 * lax.rem(z + offset, n) + core)
    for offset in range(1, n_gx):
        greet(lax.rem(gx + offset, n_gx), gy)

    def keep(d):
        return pltpu.make_async_copy(dense.at[2 * d + core], own.at[d], local_sem.at[d])

    def give(d):
        return remote(dense.at[2 * d + 1 - core], pair.at[d], pair_send.at[d], pair_recv.at[d], gx, partner)

    order = [d for t in range(n) for d in (n - 1 - t, t)][:n]
    for d in order:
        keep(d).start()
    pl.semaphore_wait(barrier, n + n_gx - 1)
    for d in order:
        give(d).start()

    def go_right(d, c):
        rows = pl.ds(c * piece, piece)
        return remote(own.at[d, rows], right.at[d, rows], right_send.at[d, c], right_recv.at[d, c], gx, gy + 2)

    def go_left(d, c):
        rows = pl.ds(c * piece, piece)
        return remote(own.at[d, rows], left.at[d, rows], left_send.at[d, c], left_recv.at[d, c], gx, gy - 2)

    def arrive(d):
        keep(d).wait()
        give(d).wait_recv()
        own[d] = own[d] + pair[d]

    def step(s, _):
        t, c = s // pieces, lax.rem(s, pieces)
        rows = pl.ds(pl.multiple_of(c * piece, 8), piece)
        far, near = n - 1 - t, t
        back = s - depth
        back_t, back_c = jnp.maximum(back, 0) // pieces, lax.rem(jnp.maximum(back, 0), pieces)

        @pl.when((back >= 0) & (z < n - 1 - back_t))
        def _():
            go_right(n - 1 - back_t, back_c).wait_send()

        @pl.when((back >= 0) & (z > back_t))
        def _():
            go_left(back_t, back_c).wait_send()

        @pl.when(z < far)
        def _():
            @pl.when(z > 0)
            def _():
                go_right(far, c).wait_recv()
                own[far, rows] = own[far, rows] + right[far, rows]

            @pl.when((s > 0) | (z > 0))
            def _():
                go_right(far, c).start()

        @pl.when(z > near)
        def _():
            @pl.when(z < n - 1)
            def _():
                go_left(near, c).wait_recv()
                own[near, rows] = own[near, rows] + left[near, rows]

            @pl.when((s > 0) | (z < n - 1))
            def _():
                go_left(near, c).start()

        return 0

    groups = n // 2
    mine = pl.ds(pl.multiple_of(core * cell_rows, 8), cell_rows)
    theirs = pl.ds(pl.multiple_of((1 - core) * cell_rows, 8), cell_rows)
    swap = remote(give_half, other, core_send.at[0], core_recv.at[0], gx, partner)
    slab = cell_rows // n_gx
    here = pl.ds(pl.multiple_of(rank * share, 8), share)

    def group_sums():
        for g in range(groups):
            give_half[g] = own[2 * g, theirs] + own[2 * g + 1, theirs]
        swap.start()
        for g in range(groups):
            half[g] = own[2 * g, mine] + own[2 * g + 1, mine]

    def across(offset):
        to = lax.rem(gx + offset, n_gx)
        rows = pl.ds(pl.multiple_of(to * slab, 8), slab)
        at = n_gx - offset - 1
        return remote(half.at[:, rows], slabs.at[at], slab_send.at[offset - 1], slab_recv.at[at], to, gy)

    def crossed(offset):
        return remote(slabs.at[offset - 1], slabs.at[offset - 1], slab_send.at[offset - 1], slab_recv.at[offset - 1], gx, partner)

    def spread():
        swap.wait_recv()
        half[...] = half[...] + other[...]
        for offset in range(1, n_gx):
            across(offset).start()

    def along(offset):
        to = lax.rem(z + offset, n)
        rows = pl.ds(pl.multiple_of(lax.rem(to, 2) * share, 8), share)
        at = n - offset - 1
        return remote(mixed.at[to // 2, rows], parts.at[at], part_send.at[offset - 1], part_recv.at[at], gx, 2 * to + core)

    def went(offset):
        return remote(parts.at[offset - 1], parts.at[offset - 1], part_send.at[offset - 1], part_recv.at[offset - 1], gx, partner)

    def descend():
        total = half[:, pl.ds(pl.multiple_of(gx * slab, 8), slab)]
        for offset in range(1, n_gx):
            crossed(offset).wait_recv()
            total = total + slabs[offset - 1]
        mixed[...] = total
        for offset in range(1, n):
            along(offset).start()

    twin = gy + 2 - 4 * lax.rem(z, 2)
    slab_rows = pl.ds(pl.multiple_of(gx * slab, 8), slab)
    pass_on = remote(full.at[here], full.at[here], core_send.at[2], core_recv.at[2], gx, twin)

    def gather(offset):
        to = lax.rem(gx + offset, n_gx)
        at = n_gx - offset - 1
        return remote(full.at[slab_rows], full.at[slab_rows], full_send.at[offset - 1], full_recv.at[at], to, gy)

    def gathered(offset):
        source = lax.rem(gx + offset, n_gx)
        rows = pl.ds(pl.multiple_of(source * slab, 8), slab)
        return remote(full.at[rows], full.at[rows], full_send.at[offset - 1], full_recv.at[offset - 1], source, gy)

    def collect():
        total = mixed[z // 2, pl.ds(pl.multiple_of(lax.rem(z, 2) * share, 8), share)]
        for offset in range(1, n):
            went(offset).wait_recv()
            total = total + parts[offset - 1]
        full[here] = total
        pass_on.start()

    def fan_out():
        other_rank = rank + 1 - 2 * lax.rem(rank, 2)
        rows = pl.ds(pl.multiple_of(other_rank * share, 8), share)
        remote(full.at[rows], full.at[rows], core_send.at[2], core_recv.at[2], gx, twin).wait_recv()
        for offset in range(1, n_gx):
            gather(offset).start()

    finish = remote(done.at[core], done.at[core], core_send.at[1], core_recv.at[1], gx, partner)
    finished = remote(done.at[1 - core], done.at[1 - core], core_send.at[1], core_recv.at[1], gx, partner)

    def project():
        for offset in range(1, n_gx):
            gathered(offset).wait_recv()
        blocks = jnp.concatenate([row for s in range(SC) for row in split_rows(tiles(full, s, SC))], axis=0)
        dot = functools.partial(jnp.dot, precision=lax.Precision.HIGHEST, preferred_element_type=F32)
        after = dot(blocks, h_ref[...])
        after = dot(ht_ref[...], jnp.concatenate([after[s * B : (s + 1) * B] for s in range(SC)], axis=1))
        for s in range(SC):
            nat[s] = after[:, s * L : (s + 1) * L]
            flat = join_rows([nat[s, pl.ds(r, G, stride=4), :] for r in range(4)])
            for m in range(3):
                done[core, pl.ds(m * SC + s, G, stride=3 * SC), :] = flat[m]
        finish.start()

    def write_last():
        finished.wait_recv()
        for u in range(cell_rows // SC):
            for r in range(RC):
                last_ref[r, :, u * L : (u + 1) * L] = done[r, u * SC : (u + 1) * SC, :]

    steps = (n - 1) * pieces
    arrive(n - 1)

    @pl.when(z == 0)
    def _():
        go_right(n - 1, 0).start()

    arrive(0)

    @pl.when(z == n - 1)
    def _():
        go_left(0, 0).start()

    for d in range(1, n - 1):
        arrive(d)
    edge = (z == 0) | (z == n - 1)
    busy = steps - pieces
    at = 0
    for stage, at_edge, between in (
        (group_sums, 2, 0),
        (spread, 4, 0),
        (descend, 9, busy),
        (collect, steps, busy),
        (fan_out, steps, busy),
        (project, steps, steps),
        (write_last, steps, steps),
    ):
        stage()
        stop = jnp.where(edge, at_edge, between)
        lax.fori_loop(at, stop, step, 0)
        at = stop

    @pl.when(z < n - 1)
    def _():
        for c in range(pieces):
            go_left(z, c).wait_recv()
        own[z] = own[z] + left[z]

    @pl.when(z > 0)
    def _():
        for c in range(pieces):
            go_right(z, c).wait_recv()
        own[z] = own[z] + right[z]

    for u in range(cell_rows // SC):
        for r in range(RC):
            first_ref[r, :, u * L : (u + 1) * L] = own[z, r * cell_rows + u * SC : r * cell_rows + (u + 1) * SC, :]

    finish.wait_send()
    swap.wait_send()
    for offset in range(1, n_gx):
        across(offset).wait_send()
    for offset in range(1, n):
        along(offset).wait_send()
    pass_on.wait_send()
    for offset in range(1, n_gx):
        gather(offset).wait_send()
    for d in range(n):
        give(d).wait_send()
    for s in range(max(steps - depth, 0), steps):
        t, c = s // pieces, s % pieces

        @pl.when(z < n - 1 - t)
        def _():
            go_right(n - 1 - t, c).wait_send()

        @pl.when(z > t)
        def _():
            go_left(t, c).wait_send()


def merge(dense, h, ht, n_gx, n_inner, flat):
    pieces, depth = 4, 4
    n = n_inner // 2
    peers = n_gx * 2
    owned = dense.shape[0] // n_inner
    cell_rows = owned // RC
    vmem = pl.BlockSpec(memory_space=pltpu.VMEM)
    dma = pltpu.SemaphoreType.DMA
    out = jax.ShapeDtypeStruct((RC, SC, flat), F32)
    return pl.pallas_call(
        functools.partial(merge_kernel, n_gx, pieces, depth),
        out_shape=(out, out),
        in_specs=[pl.BlockSpec(memory_space=pl.ANY), vmem, vmem],
        out_specs=(vmem, vmem),
        scratch_shapes=[pltpu.VMEM((n, owned, L), F32)] * 4
        + [
            pltpu.VMEM((n // 2, cell_rows, L), F32),
            pltpu.VMEM((n // 2, cell_rows, L), F32),
            pltpu.VMEM((n // 2, cell_rows, L), F32),
            pltpu.VMEM((n_gx - 1, n // 2, cell_rows // n_gx, L), F32),
            pltpu.VMEM((n // 2, cell_rows // n_gx, L), F32),
            pltpu.VMEM((n - 1, cell_rows // peers, L), F32),
            pltpu.VMEM((cell_rows, L), F32),
            pltpu.VMEM((RC, cell_rows, L), F32),
            pltpu.VMEM((SC, B, L), F32),
            dma((n,)),
            dma((n,)),
            dma((n,)),
            dma((n, pieces)),
            dma((n, pieces)),
            dma((n, pieces)),
            dma((n, pieces)),
            dma((3,)),
            dma((3,)),
            dma((n_gx - 1,)),
            dma((n_gx - 1,)),
            dma((n - 1,)),
            dma((n - 1,)),
            dma((n_gx - 1,)),
            dma((n_gx - 1,)),
        ],
        compiler_params=pltpu.CompilerParams(collective_id=0, has_side_effects=True, vmem_limit_bytes=56 * 2**20),
        cost_estimate=pl.CostEstimate(flops=4 * RC * SC * B**3, bytes_accessed=dense.size * 4, transcendentals=0),
    )(dense.reshape(n_inner, owned, L), h, ht)


def hand_over_kernel(first_in, last_in, first_ref, last_ref):
    first_ref[...] = first_in[...]
    last_ref[...] = last_in[...]


def hand_over(first, last):
    block = pl.BlockSpec((1, SC, first.shape[2]), lambda r: (r, 0, 0))
    return pl.pallas_call(
        hand_over_kernel,
        grid=(RC,),
        out_shape=(jax.ShapeDtypeStruct(first.shape, F32), jax.ShapeDtypeStruct(last.shape, F32)),
        in_specs=[block, block],
        out_specs=(block, block),
        compiler_params=pltpu.CompilerParams(vmem_limit_bytes=56 * 2**20),
    )(first, last)


def local(a_blocks, a_cols, q_blocks, part_of, part_dest, part_pos, g_level):
    n_gx, n_inner = lax.axis_size("gx"), lax.axis_size("gy")
    dense, h, ht = products(a_blocks, a_cols, q_blocks, part_of, part_dest, part_pos, g_level, n_inner)
    return hand_over(*merge(dense, h, ht, n_gx, n_inner, a_blocks.shape[2]))


def solution(mesh):
    placed = (
        P(("gx", "gy"), None, None),
        P(("gx", "gy"), None),
        P(("gx", "gy"), None),
        P(("gx", "gy"), None),
        P(("gx", "gy"), None),
        P(("gx", "gy")),
        P(),
    )
    return jax.shard_map(
        local,
        mesh=mesh,
        in_specs=placed,
        out_specs=(P(("gx", "gy"), None, None), P(("gx", "gy"), None, None)),
        check_vma=False,
    )
```
